512 devices in a mesh: patch: 32 (over y_lo, z), tensor: 16 (over y_hi, x, core).
Axes of the slice: x: 4, y: 4 (y_hi: 2, y_lo: 2; y = y_hi * 2 + y_lo), z: 16, core: 2. Of those that a mesh axis runs over, the one named last changes fastest.
Arguments:
- inputs: bfloat16 [24576, 1024], P('patch'), may hold values from -22.5 to 22.5
- cotangent: bfloat16 [24576, 1024], P('patch'), may hold values from -6 to 6
- norm_gain: float32 [1024], replicated, may hold values from 0.5 to 1.5
- proj_weight: bfloat16 [1024, 4, 1024], P(None, None, 'tensor'), may hold values from -2 to 2
- weight_noise: bfloat16 [1024, 4, 1024], P(None, None, 'tensor'), may hold values from -0.09375 to 0.09375
- patch_counts: int32 [32], replicated, may hold values from 1 to 12, as said below
- neighbours: int32 [384, 9], P('patch'), may hold values from -1 to 35, as said below
- pixel_valid: int32 [384, 64], replicated, may hold values from 0 to 1, as said below
Outputs:
- input_grad: bfloat16 [24576, 1024], P('patch', 'tensor')
- proj_grads: float32 [1024, 4, 1024], P('patch', None, 'tensor')
The draws below stay inside these ranges and needn't reach their ends.
Inputs may be any that keep to these rules, and one draw needn't show every extreme that they name: `patch_counts`: some device other than the first holds exactly 12 patches. `neighbours`: each row lists the slot itself first, then up to 8 other distinct slots, -1 marking an absent entry; entries index the 36 slots of the previous, own and next device and name only slots below that device's count; a slot at or above its device's count lists only itself. `pixel_valid`: every patch has a valid pixel.
All inputs are finite; a program needn't handle non-finite values.
Results may differ from the reference program's by a relative error of at most 0.03.
The reference program's roundings to bfloat16 on the way (of `upstream`, `hidden`, `weights`, `attention_bf`, `attended`, `out_grad`, `score_grad` and `query_grad`) count: a program that leaves them out, or rounds other values in their place, can miss the bound.
Values may be sent and summed in bfloat16 or wider, within the bound.
A program may use at most 64 MiB of HBM per device.

```python
import jax
import jax.numpy as jnp
from jax import lax

D = 1024
HS = 64
PIX = 64
NB = 9
CAP = 12
HEADS = 16
HH = 1024
SLOTS = 384
ROWS = 24576
N_PATCH = 32


def slot_counts(key):
    first, second = jax.random.split(key)
    counts = jax.random.randint(first, (N_PATCH,), 1, CAP + 1)
    fullest = jax.random.randint(second, (), 1, N_PATCH)
    return jnp.where(jnp.arange(N_PATCH) == fullest, CAP, counts).astype(jnp.int32)


def draw_patch_counts(key, part):
    return slot_counts(key)


def draw_neighbours(key, part):
    counts = slot_counts(key)
    key = jax.random.fold_in(key, 7)
    first, second = jax.random.split(key)
    slot_ids = jnp.arange(SLOTS).astype(jnp.int32)
    device_of = slot_ids // CAP
    own_index = slot_ids % CAP
    offsets = jnp.arange(3 * CAP).astype(jnp.int32)
    window_device = device_of[:, None] - 1 + offsets[None, :] // CAP
    window_slot = (offsets % CAP)[None, :]
    inside = (window_device >= 0) & (window_device < N_PATCH)
    window_count = counts[jnp.clip(window_device, 0, N_PATCH - 1)]
    usable = inside & (window_slot < window_count) & (offsets[None, :] != CAP + own_index[:, None])
    random_part = jax.random.randint(first, (SLOTS, 3 * CAP), 0, 2 ** 20)
    score = random_part * (3 * CAP) + offsets[None, :]
    score = jnp.where(usable, score, -1 - offsets[None, :])
    kept = min(NB - 1, 3 * CAP - 1)
    top_values, top_index = lax.top_k(score, kept)
    extra = jax.random.randint(second, (SLOTS, 1), NB - 3, NB)
    position = jnp.arange(kept)[None, :]
    live_slot = (own_index < counts[device_of])[:, None]
    chosen = (top_values >= 0) & (position < extra) & live_slot
    others = jnp.where(chosen, top_index, -1)
    self_column = (CAP + own_index)[:, None]
    filler = -jnp.ones((SLOTS, NB - 1 - kept), jnp.int32)
    return jnp.concatenate([self_column, others.astype(jnp.int32), filler], axis=1).astype(jnp.int32)


def draw_pixel_valid(key, part):
    key = jax.random.fold_in(key, 9)
    first, second = jax.random.split(key)
    keep = jax.random.randint(first, (SLOTS, PIX), 0, 8) < 7
    forced = jax.random.randint(second, (SLOTS, 1), 0, PIX)
    return (keep | (jnp.arange(PIX)[None, :] == forced)).astype(jnp.int32)


def draw_inputs(key, part):
    key = jax.random.fold_in(key, 13)
    keys = jax.random.split(key, 3)
    row_scale = jnp.exp(jax.random.uniform(keys[0], (ROWS, 1)) * jnp.log(10.0))
    column_scale = jnp.exp(jax.random.uniform(keys[1], (1, D)) * jnp.log(10.0))
    values = jnp.clip(jax.random.normal(keys[2], (ROWS, D)), -4.0, 4.0)
    return (0.05 * values * row_scale * column_scale).astype(jnp.bfloat16)


def draw_proj_weight(key, part):
    key = jax.random.fold_in(key, 17)
    scale = D ** (-0.5)
    values = jnp.clip(jax.random.normal(key, (D, 4, HH)), -4.0, 4.0) * scale
    return jnp.clip(values, -2.0, 2.0).astype(jnp.bfloat16)


def spiked(array, own_key, source, target, parts, factor):
    owner, partner = [(jnp.arange(array.shape[axis_at]) // (array.shape[axis_at] // parts)).reshape([-1 if axis == axis_at else 1 for axis in range(array.ndim)]) for axis_at in (source, target)]
    chosen = jax.random.permutation(own_key, parts)[partner]
    strong = (owner == chosen) | (owner == (partner + parts // 2) % parts)
    return jnp.where(strong, factor * array, array)


def shard_levels(stream_key, shape, cuts, least, high):
    factor_of, own = 1.0, jax.random.fold_in(stream_key, 6)
    for dim, shards_of in cuts:
        heights = jnp.exp(jax.random.uniform(jax.random.fold_in(own, dim), (shards_of,), jnp.float32, least / len(cuts), high / len(cuts)))
        factor_of = factor_of * jnp.repeat(heights, shape[dim] // shards_of).reshape([-1 if axis == dim else 1 for axis in range(len(shape))])
    return factor_of


def normal_values(own_key, extent, deviation, bound, shards=(), kind=jnp.bfloat16):
    gain = shard_levels(own_key, extent, shards, -0.22, 0.18) if shards else 1.0
    values = jax.random.normal(own_key, extent, jnp.float32) * deviation * gain
    return jnp.minimum(jnp.maximum(values, -bound), bound).astype(kind)


def gaussian_with(stream_key, dims, deviation, reach, cuts, heavy, kind=jnp.bfloat16):
    entries = deviation * jax.random.normal(stream_key, dims, jnp.float32)
    if cuts:
        entries = entries * shard_levels(stream_key, dims, cuts, -0.22, 0.18)
    return jnp.clip(spiked(entries, jax.random.fold_in(stream_key, 3), *heavy), -reach, reach).astype(kind)


def setup_inputs(seed: int = 0) -> dict:
    streams_of = jax.random.split(jax.random.key(seed), 9)
    return {
        "inputs": draw_inputs(jax.random.fold_in(streams_of[8], 71), 0),
        "cotangent": gaussian_with(streams_of[1], (ROWS, D), 1.0, 6.0, ((0, 32),), (0, 1, 32, 2.75)),
        "norm_gain": jnp.clip(1.0 + 0.1 * jax.random.normal(streams_of[2], (D,), jnp.float32), 0.5, 1.5),
        "proj_weight": draw_proj_weight(jax.random.fold_in(streams_of[8], 71), 0),
        "weight_noise": normal_values(streams_of[4], (D, 4, HH), (4 * D) ** -0.5, 0.09375, ((2, 16),)),
        "patch_counts": draw_patch_counts(jax.random.fold_in(streams_of[8], 71), 0),
        "neighbours": draw_neighbours(jax.random.fold_in(streams_of[8], 71), 0),
        "pixel_valid": draw_pixel_valid(jax.random.fold_in(streams_of[8], 71), 0),
    }


def rms_parts(inputs, norm_gain):
    values = inputs.astype(jnp.float32)
    inverse_rms = lax.rsqrt(lax.optimization_barrier(jnp.mean(values * values, axis=1, keepdims=True)) + 1e-06)
    normed = values * inverse_rms
    hidden = (normed * norm_gain.astype(jnp.float32)).astype(jnp.bfloat16)
    return (inverse_rms, normed, hidden)

def reference(inputs, cotangent, norm_gain, proj_weight, weight_noise, patch_counts, neighbours, pixel_valid):
    inverse_rms, normed, hidden = rms_parts(inputs, norm_gain)
    weights = (proj_weight.astype(jnp.float32) + weight_noise.astype(jnp.float32)).astype(jnp.bfloat16)
    slot_ids = jnp.arange(SLOTS).astype(jnp.int32)
    device_of = slot_ids // CAP
    live_slot = slot_ids % CAP < patch_counts[device_of]
    live_rows = jnp.repeat(live_slot, PIX)
    upstream = jnp.where(live_rows[:, None], cotangent, jnp.zeros_like(cotangent))
    present = neighbours >= 0
    global_slot = jnp.where(present, (device_of[:, None] - 1) * CAP + neighbours, 0).astype(jnp.int32)
    key_valid = ((pixel_valid[global_slot] > 0) & present[:, :, None]).reshape(SLOTS, NB * PIX)
    factor = HS ** (-0.5)

    def one_head(carry, head_index):
        block = lax.dynamic_slice_in_dim(weights, head_index * HS, HS, 2)
        in_weights = block[:, :3].reshape(D, 3 * HS)
        projected = jnp.dot(hidden, in_weights, preferred_element_type=jnp.float32).astype(jnp.bfloat16)
        queries = projected[:, :HS].reshape(SLOTS, PIX, HS).astype(jnp.float32)
        keys_all = projected[:, HS:2 * HS].reshape(SLOTS, PIX, HS)
        values_all = projected[:, 2 * HS:].reshape(SLOTS, PIX, HS)
        near_keys = keys_all[global_slot].reshape(SLOTS, NB * PIX, HS).astype(jnp.float32)
        near_values = values_all[global_slot].reshape(SLOTS, NB * PIX, HS).astype(jnp.float32)
        scores = jnp.einsum('spd,skd->spk', queries, near_keys) * factor
        scores = jnp.where(key_valid[:, None, :], scores, -jnp.inf)
        row_max = lax.optimization_barrier(jnp.max(scores, axis=2, keepdims=True))
        exponent = jnp.exp(scores - row_max)
        attention = exponent / lax.optimization_barrier(jnp.sum(exponent, axis=2, keepdims=True))
        attention_bf = attention.astype(jnp.bfloat16).astype(jnp.float32)
        attended = jnp.einsum('spk,skd->spd', attention_bf, near_values).astype(jnp.bfloat16).reshape(ROWS, HS)
        out_grad = jnp.dot(upstream, block[:, 3], preferred_element_type=jnp.float32).astype(jnp.bfloat16)
        out_grad3 = out_grad.reshape(SLOTS, PIX, HS).astype(jnp.float32)
        prob_grad = jnp.einsum('spd,skd->spk', out_grad3, near_values)
        value_near = jnp.einsum('spk,spd->skd', attention_bf, out_grad3)
        score_grad = (attention * (prob_grad - lax.optimization_barrier(jnp.sum(attention * prob_grad, axis=2, keepdims=True))) * factor).astype(jnp.bfloat16).astype(jnp.float32)
        query_grad = jnp.einsum('spk,skd->spd', score_grad, near_keys).astype(jnp.bfloat16).reshape(ROWS, HS)
        key_near = jnp.einsum('spk,spd->skd', score_grad, queries)
        near_grad = jnp.concatenate([key_near, value_near], axis=2).reshape(SLOTS, NB, PIX, 2 * HS)
        near_grad = jnp.where(present[:, :, None, None], near_grad, 0.0)
        slot_grad = jnp.zeros((SLOTS, PIX, 2 * HS), jnp.float32).at[global_slot].add(near_grad)
        key_value_grad = slot_grad.reshape(ROWS, 2 * HS).astype(jnp.bfloat16)
        grads = jnp.concatenate([query_grad, key_value_grad], axis=1)
        part = jnp.dot(grads, in_weights.T, preferred_element_type=jnp.float32).astype(jnp.bfloat16)
        part = lax.optimization_barrier(part)
        carry = carry + part.astype(jnp.float32)
        in_grad = jnp.dot(hidden.T, grads, preferred_element_type=jnp.float32).reshape(D, 3, HS)
        out_weight_grad = jnp.dot(upstream.T, attended, preferred_element_type=jnp.float32)
        return (carry, jnp.concatenate([in_grad, out_weight_grad[:, None, :]], axis=1))
    start = jnp.zeros((ROWS, D), jnp.float32)
    feature_grad, head_grads = lax.scan(one_head, start, jnp.arange(HEADS).astype(jnp.int32))
    scaled = feature_grad * norm_gain.astype(jnp.float32)
    mean_term = lax.optimization_barrier(jnp.mean(scaled * normed, axis=1, keepdims=True))
    input_grad = (upstream.astype(jnp.float32) + inverse_rms * (scaled - normed * mean_term)).astype(jnp.bfloat16)
    proj_grads = jnp.transpose(head_grads, (1, 2, 0, 3)).reshape(D, 4, HH)
    return (input_grad, proj_grads)
```

```python
import jax
import jax.numpy as jnp
from jax import lax
from jax.experimental import pallas as pl
from jax.experimental.pallas import tpu as pltpu
from jax.sharding import PartitionSpec as P

BF = jnp.bfloat16
F32 = jnp.float32
MESH = pl.DeviceIdType.MESH
OFF = -1e30

ROWS = 768
D = 1024
PIX = 64
CAP = 12
NB = 9
TILE = 256
Z = 16
NX = 4


def nn(a, b):
    return lax.dot_general(a, b, (((1,), (0,)), ((), ())), preferred_element_type=F32)


def nt(a, b):
    return lax.dot_general(a, b, (((1,), (1,)), ((), ())), preferred_element_type=F32)


def tile(i, size=TILE):
    if isinstance(i, int):
        return pl.ds(i * size, size)
    return pl.ds(pl.multiple_of(i * size, size), size)


def remote(src, dst, send_sem, recv_sem, **device):
    return pltpu.make_async_remote_copy(
        src_ref=src,
        dst_ref=dst,
        send_sem=send_sem,
        recv_sem=recv_sem,
        device_id=device,
        device_id_type=MESH,
    )


def kernel(
    x_ref, g_ref, gain_ref, w_ref, counts_ref, nb_ref, pv_ref,
    og_ref, pg_ref,
    hid, up, irms, nshare, ushare, kvw, kvt, kaug, qaug, qz, dz, q_t,
    sc, dp, mx, pt, ds_t, halo_out, own_grad, halo_in, att_t, grads_t,
    m_out, m_in, pj, y_in, z_out, z_in,
    part, r1, s2, r2, r3, s3, r4,
    halo_s, halo_r, hg_s, hg_r, m_s, m_r, y_s, y_r, z_s, z_r,
    c_s, c_r, r2_s, r2_r, r3_s, r3_r, r4_s, r4_r,
):
    p = lax.axis_index("patch")
    t = lax.axis_index("tensor")
    y_lo, z = p // Z, p % Z
    core = t % 2
    x = (t // 2) % NX
    y_hi = t // 8
    right, left = (p + 1) % 32, (p + 31) % 32
    y_partner = (1 - y_lo) * Z + z
    row0 = t - x * 2
    x_right, x_left = row0 + ((x + 1) % NX) * 2, row0 + ((x + 3) % NX) * 2
    core_partner = t + 1 - 2 * core
    hi_partner = (t + 8) % 16

    def z_peer(r):
        return y_lo * Z + (z + r) % Z

    barrier = pltpu.get_barrier_semaphore()

    def greet(r, carry):
        pl.semaphore_signal(barrier, inc=1, device_id={"patch": z_peer(r)}, device_id_type=MESH)
        pl.semaphore_signal(barrier, inc=1, device_id={"tensor": (t + r) % 16}, device_id_type=MESH)
        return carry

    lax.fori_loop(1, 16, greet, 0)
    for other in (left, right, y_partner):
        pl.semaphore_signal(barrier, inc=1, device_id={"patch": other}, device_id_type=MESH)

    gain = gain_ref[...]

    def project(i, carry):
        rows = tile(i)
        xs = x_ref[rows, :].astype(F32)
        inv = lax.rsqrt(jnp.sum(xs * xs, axis=1, keepdims=True) * (1.0 / D) + 1e-06)
        h = (xs * inv * gain).astype(BF)
        hid[rows, :] = h
        irms[rows, :] = jnp.broadcast_to(inv, (TILE, 128))
        pr = nn(h, w_ref[...])
        kvw[1, rows, :] = pr[:, :128].astype(BF)
        lane = lax.broadcasted_iota(jnp.int32, (TILE, 128), 1)
        q = jnp.where(lane < 64, pr[:, 128:].astype(BF).astype(F32), 0.0)
        qz[rows, :] = (q * 0.125).astype(BF)
        q_t[:, rows] = jnp.transpose(q)[:64, :].astype(BF)
        return carry

    lax.fori_loop(0, 3, project, 0)

    pl.semaphore_wait(barrier, 33)
    to_next = remote(kvw.at[1], kvw.at[0], halo_s.at[0], halo_r.at[0], patch=right)
    to_prev = remote(kvw.at[1], kvw.at[2], halo_s.at[1], halo_r.at[1], patch=left)
    to_next.start()
    to_prev.start()

    lane12 = lax.broadcasted_iota(jnp.int32, (CAP, 128), 1)
    nb = nb_ref[...]
    member = lane12 == 64 + nb[:, 0:1]
    for j in range(1, NB):
        member = member | (lane12 == 64 + nb[:, j : j + 1])
    member = jnp.where(member, 0.0, OFF)
    member = jnp.where(lane12 == 100, 1.0, jnp.where(lane12 > 100, 0.0, member))
    lane64 = lax.broadcasted_iota(jnp.int32, (PIX, 128), 1)
    row64 = lax.broadcasted_iota(jnp.int32, (PIX, PIX), 0)
    col64 = lax.broadcasted_iota(jnp.int32, (PIX, PIX), 1)
    for b, owner in enumerate((left, p, right)):
        valid = jnp.where(pv_ref[pl.ds(owner * CAP, CAP), :] > 0, 0.0, OFF)
        for s in range(CAP):
            off = jnp.sum(
                jnp.where(row64 == col64, valid[s : s + 1, :], 0.0), axis=1, keepdims=True
            )
            aux = jnp.where(lane64 == 64 + b * CAP + s, 1.0, 0.0)
            aux = jnp.where(lane64 == 100, off, aux)
            kaug[b, s * PIX : (s + 1) * PIX, :] = aux.astype(BF)

    live = counts_ref[p] * PIX

    def upstream(i, carry):
        rows = tile(i)
        row = lax.broadcasted_iota(jnp.int32, (TILE, 1), 0) + i * TILE
        g = jnp.where(row < live, g_ref[rows, :].astype(F32), 0.0).astype(BF)
        up[rows, :] = g
        og = nn(g, w_ref[:, 128:])
        lane = lax.broadcasted_iota(jnp.int32, (TILE, 128), 1)
        dz[rows, :] = jnp.where(lane >= 64, og, 0.0).astype(BF)
        return carry

    lax.fori_loop(0, 3, upstream, 0)
    for s in range(CAP):
        rows = slice(s * PIX, (s + 1) * PIX)
        qaug[rows, :] = jnp.where(lane64 < 64, qz[rows, :].astype(F32), member[s : s + 1, :]).astype(BF)

    mx[...] = jnp.full_like(mx, 2.0 * OFF)

    def score(b):
        def step(i, carry):
            rows = tile(i)
            lane = lax.broadcasted_iota(jnp.int32, (TILE, 128), 1)
            kv = kvw[b, rows, :]
            ka = jnp.where(lane < 64, kv.astype(F32), kaug[b, rows, :].astype(F32)).astype(BF)
            kvt[b, :, rows] = jnp.transpose(kv.astype(F32)).astype(BF)
            at = tile(b * 3 + i)
            for q in range(3):
                cols = tile(q)
                s = nt(ka, qaug[cols, :])
                sc[at, cols] = s
                mx[:, cols] = jnp.maximum(mx[:, cols], jnp.max(s.reshape(32, 8, TILE), axis=0))
                dp[at, cols] = nt(kv, dz[cols, :])
            return carry

        lax.fori_loop(0, 3, step, 0)

    score(1)

    odd = core == 1
    share = pl.ds(pl.multiple_of((t // 2) * 128, 128), 128)
    gain_share = gain_ref[:, share]
    gain_share = jnp.where(odd, pltpu.roll(gain_share, 64, 1), gain_share)

    def shares(i, carry):
        rows = tile(i)
        xs = x_ref[rows, share].astype(F32)
        nshare[rows, :] = jnp.where(odd, pltpu.roll(xs, 64, 1), xs) * irms[rows, :]
        us = up[rows, share].astype(F32)
        ushare[rows, :] = jnp.where(odd, pltpu.roll(us, 64, 1), us)
        return carry

    lax.fori_loop(0, 3, shares, 0)

    to_next.wait_recv()
    score(0)
    to_prev.wait_recv()
    score(2)

    def soften(q, carry):
        cols = tile(q)
        top = jnp.max(mx[:, cols], axis=0, keepdims=True)

        def first(i, sums):
            total, weighted = sums
            rows = tile(i)
            e = jnp.exp(sc[rows, cols] - top)
            sc[rows, cols] = e
            total = total + jnp.sum(e.reshape(32, 8, TILE), axis=0)
            weighted = weighted + jnp.sum((e * dp[rows, cols]).reshape(32, 8, TILE), axis=0)
            return total, weighted

        zero = jnp.zeros((8, TILE), F32)
        total, weighted = lax.fori_loop(0, 9, first, (zero, zero))
        inv = 1.0 / jnp.sum(total, axis=0, keepdims=True)
        delta = jnp.sum(weighted, axis=0, keepdims=True) * inv

        def second(i, carry):
            rows = tile(i)
            att = sc[rows, cols] * inv
            pt[rows, cols] = att.astype(BF)
            ds_t[rows, cols] = (att * (dp[rows, cols] - delta)).astype(BF)
            return carry

        lax.fori_loop(0, 9, second, 0)
        return carry

    lax.fori_loop(0, 3, soften, 0)

    def near_grad(b, i):
        at = tile(b * 3 + i)
        return nn(ds_t[at, :], qz[...]) + nn(pt[at, :], dz[...])

    def halo_grad(b, slot):
        def step(i, carry):
            halo_out[slot, tile(i), :] = near_grad(b, i).astype(BF)
            return carry

        lax.fori_loop(0, 3, step, 0)

    halo_grad(0, 0)
    grad_prev = remote(halo_out.at[0], halo_in.at[1], hg_s.at[0], hg_r.at[0], patch=left)
    grad_prev.start()
    halo_grad(2, 1)
    grad_next = remote(halo_out.at[1], halo_in.at[0], hg_s.at[1], hg_r.at[1], patch=right)
    grad_next.start()

    def own(i, carry):
        own_grad[tile(i), :] = near_grad(1, i)
        return carry

    lax.fori_loop(0, 3, own, 0)

    def query_side(q, carry):
        cols = tile(q)
        qg = jnp.zeros((64, TILE), F32)
        at = jnp.zeros((64, TILE), F32)
        for b in range(3):
            rows = slice(b * ROWS, (b + 1) * ROWS)
            qg = qg + nn(kvt[b, 0:64, :], ds_t[rows, cols])
            at = at + nn(kvt[b, 64:128, :], pt[rows, cols])
        grads_t[128:192, cols] = (qg * 0.125).astype(BF)
        att_t[:, cols] = at.astype(BF)
        return carry

    lax.fori_loop(0, 3, query_side, 0)

    def weight_qo(n, carry):
        cols = tile(n)
        both = jnp.concatenate(
            [nn(grads_t[128:192, :], hid[:, cols]), nn(att_t[...], up[:, cols])], axis=0
        )
        pj[0, cols, :] = jnp.transpose(both).astype(BF)
        return carry

    lax.fori_loop(0, 4, weight_qo, 0)

    def y_copy(h):
        return remote(
            pj.at[h, tile(1 - y_lo, 512), :], y_in.at[h], y_s.at[h], y_r.at[h], patch=y_partner
        )

    y_copy(0).start()

    grad_next.wait_recv()
    grad_prev.wait_recv()

    def collect(i, carry):
        rows = tile(i)
        total = (
            own_grad[rows, :] + halo_in[0, rows, :].astype(F32) + halo_in[1, rows, :].astype(F32)
        )
        kvg = jnp.transpose(total).astype(BF)
        grads_t[0:128, rows] = kvg
        prod = jnp.sum(kvg.astype(F32) * kvt[1, :, rows].astype(F32), axis=0, keepdims=True)
        qg = grads_t[128:192, rows].astype(F32) * q_t[:, rows].astype(F32)
        prod = prod + jnp.sum(qg, axis=0, keepdims=True)
        for j in range(2):
            m_out[pl.ds(2 * i + j, 1), :] = prod[:, j * 128 : (j + 1) * 128]
        return carry

    m_out[...] = jnp.zeros_like(m_out)
    lax.fori_loop(0, 3, collect, 0)

    def m_send(r, carry):
        remote(m_out, m_in.at[r - 1], m_s, m_r, tensor=(t + r) % 16).start()
        return carry

    lax.fori_loop(1, 16, m_send, 0)

    order = [(2, 0), (2, 1), (1, 0), (3, 0), (0, 0), (1, 1), (3, 1), (0, 1)]

    def block_of(o):
        dx, k = order[o]
        y = (1 - y_hi) if k == 0 else y_hi
        return y * NX + (x + dx) % NX

    def core_copy(o):
        return remote(
            part.at[o, tile(1 - core, 64), :], r1.at[o], c_s.at[o], c_r.at[o], tensor=core_partner
        )

    for o in range(8):
        rows = tile(block_of(o), 128)
        part[o] = nn(w_ref[rows, 0:192], grads_t[...]).astype(BF)
        core_copy(o).start()

    def weight_kv(n, carry):
        cols = tile(n)
        pj[1, cols, :] = jnp.transpose(nn(grads_t[0:128, :], hid[:, cols])).astype(BF)
        return carry

    lax.fori_loop(0, 4, weight_kv, 0)
    y_copy(1).start()

    def pair_sum(o):
        core_copy(o).wait_recv()
        return part[o, tile(core, 64), :].astype(F32) + r1[o].astype(F32)

    def r2_copy(k, side):
        half = slice(side * 32, side * 32 + 32)
        return remote(
            s2.at[k, half, :], r2.at[side, k], r2_s.at[side, k], r2_r.at[side, k],
            tensor=x_right if side == 0 else x_left,
        )

    def r3_copy(k, side, half):
        o = 2 + 3 * k + side
        rows = slice(half * 32, half * 32 + 32)
        return remote(
            s2.at[o, rows, :], r3.at[side, k, rows, :], r3_s.at[side, k, half], r3_r.at[side, k, half],
            tensor=x_right if side == 0 else x_left,
        )

    def z_copy(h, r):
        return remote(
            z_out.at[h, tile((z + r) % Z, 32), :], z_in.at[h, r - 1], z_s.at[h], z_r.at[h],
            patch=z_peer(r),
        )

    def z_stage(h):
        y_copy(h).wait_recv()
        z_out[h] = (
            pj[h, tile(y_lo, 512), :].astype(F32) + y_in[h].astype(F32)
        ).astype(BF)

        def step(r, carry):
            z_copy(h, r).start()
            return carry

        lax.fori_loop(1, Z, step, 0)

    for k in range(2):
        s2[k] = pair_sum(k).astype(BF)
        for side in range(2):
            r2_copy(k, side).start()
    for k in range(2):
        for side in range(2):
            o = 2 + 3 * k + side
            s2[o] = pair_sum(o).astype(BF)
            r3_copy(k, side, 1 - side).start()
    z_stage(0)
    for k in range(2):
        for side in range(2):
            o = 2 + 3 * k + side
            half = slice(side * 32, side * 32 + 32)
            r2_copy(k, side).wait_recv()
            s2[o, half, :] = (
                pair_sum_again(part, r1, core, o, half) + r2[side, k].astype(F32)
            ).astype(BF)
            r3_copy(k, side, side).start()
    z_stage(1)

    def x_sum(k):
        o = 4 + 3 * k
        total = pair_sum(o)
        for side in range(2):
            for half in range(2):
                r3_copy(k, side, half).wait_recv()
            total = total + r3[side, k].astype(F32)
        return total

    r4_copy = remote(s3, r4, r4_s, r4_r, tensor=hi_partner)
    s3[...] = x_sum(0).astype(BF)
    r4_copy.start()
    feature = x_sum(1)

    for h in range(2):
        pltpu.make_async_copy(z_in.at[h], z_in.at[h], z_r.at[h]).wait()
        total = z_out[h, tile(z, 32), :].astype(F32)
        for r in range(Z - 1):
            total = total + z_in[h, r].astype(F32)
        pg_ref[h] = total

    pltpu.make_async_copy(m_in, m_in, m_r).wait()
    m = m_out[...]
    for r in range(15):
        m = m + m_in[r]
    m = m * (1.0 / D)
    mean = jnp.concatenate([m[i : i + 1, :] for i in range(6)], axis=1)

    r4_copy.wait_recv()
    feature = feature + r4[...].astype(F32)
    both = jnp.concatenate([feature, jnp.broadcast_to(mean, (64, ROWS))], axis=0)
    for i in range(3):
        rows = slice(i * TILE, (i + 1) * TILE)
        turned = jnp.transpose(both[:, rows])
        means = pltpu.roll(turned, 64, 1)
        grad = ushare[rows, :] + irms[rows, :] * (turned * gain_share - nshare[rows, :] * means)
        og_ref[rows, :] = grad[:, :64].astype(BF)

    to_next.wait_send()
    to_prev.wait_send()
    grad_prev.wait_send()
    grad_next.wait_send()
    for o in range(8):
        core_copy(o).wait_send()
    for k in range(2):
        for side in range(2):
            r2_copy(k, side).wait_send()
            for half in range(2):
                r3_copy(k, side, half).wait_send()
    r4_copy.wait_send()
    for h in range(2):
        y_copy(h).wait_send()
        pltpu.make_async_copy(z_in.at[h], z_in.at[h], z_s.at[h]).wait()
    pltpu.make_async_copy(m_in, m_in, m_s).wait()


def pair_sum_again(part, r1, core, o, half):
    rows = pl.ds(pl.multiple_of(core * 64 + half.start, 32), 32)
    return part[o, rows, :].astype(F32) + r1[o, half, :].astype(F32)


def per_device(
    inputs, cotangent, norm_gain, proj_weight, weight_noise, patch_counts, neighbours, pixel_valid
):
    weights = (proj_weight.astype(F32) + weight_noise.astype(F32)).astype(BF)
    weights = jnp.concatenate(
        [weights[:, 1], weights[:, 2], weights[:, 0], weights[:, 3]], axis=1
    )
    vmem = pl.BlockSpec(memory_space=pltpu.VMEM)
    smem = pl.BlockSpec(memory_space=pltpu.SMEM)
    V = pltpu.VMEM
    dma = pltpu.SemaphoreType.DMA
    grad, proj = pl.pallas_call(
        kernel,
        out_shape=(
            jax.ShapeDtypeStruct((ROWS, 64), BF),
            jax.ShapeDtypeStruct((2, 32, 128), F32),
        ),
        in_specs=[vmem, vmem, vmem, vmem, smem, vmem, vmem],
        out_specs=(vmem, vmem),
        scratch_shapes=[
            V((ROWS, D), BF),
            V((ROWS, D), BF),
            V((ROWS, 128), F32),
            V((ROWS, 128), F32),
            V((ROWS, 128), F32),
            V((3, ROWS, 128), BF),
            V((3, 128, ROWS), BF),
            V((3, ROWS, 128), BF),
            V((ROWS, 128), BF),
            V((ROWS, 128), BF),
            V((ROWS, 128), BF),
            V((64, ROWS), BF),
            V((3 * ROWS, ROWS), F32),
            V((3 * ROWS, ROWS), F32),
            V((8, ROWS), F32),
            V((3 * ROWS, ROWS), BF),
            V((3 * ROWS, ROWS), BF),
            V((2, ROWS, 128), BF),
            V((ROWS, 128), F32),
            V((2, ROWS, 128), BF),
            V((64, ROWS), BF),
            V((192, ROWS), BF),
            V((8, 128), F32),
            V((15, 8, 128), F32),
            V((2, D, 128), BF),
            V((2, 512, 128), BF),
            V((2, 512, 128), BF),
            V((2, 15, 32, 128), BF),
            V((8, 128, ROWS), BF),
            V((8, 64, ROWS), BF),
            V((8, 64, ROWS), BF),
            V((2, 2, 32, ROWS), BF),
            V((2, 2, 64, ROWS), BF),
            V((64, ROWS), BF),
            V((64, ROWS), BF),
            dma((2,)), dma((2,)),
            dma((2,)), dma((2,)),
            dma, dma,
            dma((2,)), dma((2,)),
            dma((2,)), dma((2,)),
            dma((8,)), dma((8,)),
            dma((2, 2)), dma((2, 2)),
            dma((2, 2, 2)), dma((2, 2, 2)),
            dma, dma,
        ],
        compiler_params=pltpu.CompilerParams(
            collective_id=0, has_side_effects=True, vmem_limit_bytes=56 * 1024 * 1024
        ),
        cost_estimate=pl.CostEstimate(
            flops=4 * 10**9, bytes_accessed=5 * 10**6, transcendentals=2 * 10**6
        ),
    )(
        inputs,
        cotangent,
        norm_gain.reshape(1, D),
        weights,
        patch_counts,
        neighbours,
        pixel_valid,
    )
    proj = jnp.stack([proj[0, :, :64], proj[1, :, :64], proj[1, :, 64:], proj[0, :, 64:]], axis=1)
    return (grad, proj)


def solution(mesh):
    placed = (
        P("patch", None),
        P("patch", None),
        P(),
        P(None, None, "tensor"),
        P(None, None, "tensor"),
        P(),
        P("patch", None),
        P(),
    )
    return jax.shard_map(
        per_device,
        mesh=mesh,
        in_specs=placed,
        out_specs=(P("patch", "tensor"), P("patch", None, "tensor")),
        check_vma=False,
    )
```

```python
import jax
import jax.numpy as jnp
from jax import lax
from jax.experimental import pallas as pl
from jax.experimental.pallas import tpu as pltpu
from jax.sharding import PartitionSpec as P

BF = jnp.bfloat16
F32 = jnp.float32
MESH = pl.DeviceIdType.MESH
OFF = -1e30

ROWS = 768
D = 1024
PIX = 64
CAP = 12
NB = 9
TILE = 256
HALF = 384
Z = 16
SLOTS = 384
Z_STEPS = (1, 15, 2, 14, 4, 8, 12)
NX = 4


def nn(a, b):
    return lax.dot_general(a, b, (((1,), (0,)), ((), ())), preferred_element_type=F32)


def nt(a, b):
    return lax.dot_general(a, b, (((1,), (1,)), ((), ())), preferred_element_type=F32)


def tile(i, size=TILE):
    if isinstance(i, int):
        return pl.ds(i * size, size)
    return pl.ds(pl.multiple_of(i * size, size), size)


def remote(src, dst, send_sem, recv_sem, **device):
    return pltpu.make_async_remote_copy(
        src_ref=src,
        dst_ref=dst,
        send_sem=send_sem,
        recv_sem=recv_sem,
        device_id=device,
        device_id_type=MESH,
    )


def kernel(
    x_hbm, g_hbm, gain_hbm, pw_hbm, wn_hbm, counts_ref, nb_hbm, pv_hbm,
    og_ref, pg_ref,
    x_ref, g_ref, gain_ref, pw_ref, wn_ref, nb_ref, pv_ref, wt, wk, hid, up, irms, fscale, nshare, ushare, kvw, kvt, kaug, qaug, qz, dz, q_t,
    sc, dp, mx, sums, pt, ds_t, halo_out, own_grad, halo_in, att_t, grads_t,
    m_out, m_in, pj, y_in, z_out, z_in, zb_out, zb_in,
    part, r1, s2, r2, r3, s3, r4,
    x_s, g_s, w_s, halo_s, halo_r, hg_s, hg_r, m_s, m_r, y_s, y_r, za_s, za_r, zb_s, zb_r,
    c_s, c_r, r2_s, r2_r, r3_s, r3_r, r4_s, r4_r,
):
    p = lax.axis_index("patch")
    t = lax.axis_index("tensor")
    y_lo, z = p // Z, p % Z
    core = t % 2
    x = (t // 2) % NX
    y_hi = t // 8
    right, left = (p + 1) % 32, (p + 31) % 32
    y_partner = (1 - y_lo) * Z + z
    row0 = t - x * 2
    x_right, x_left = row0 + ((x + 1) % NX) * 2, row0 + ((x + 3) % NX) * 2
    core_partner = t + 1 - 2 * core
    hi_partner = (t + 8) % 16

    def z_peer(r):
        return y_lo * Z + (z + r) % Z

    loads = [
        pltpu.make_async_copy(pw_hbm, pw_ref, w_s.at[0]),
        pltpu.make_async_copy(wn_hbm, wn_ref, w_s.at[1]),
        pltpu.make_async_copy(gain_hbm, gain_ref, w_s.at[2]),
    ]
    late_loads = [
        pltpu.make_async_copy(nb_hbm, nb_ref, w_s.at[3]),
        pltpu.make_async_copy(pv_hbm, pv_ref, w_s.at[4]),
        pltpu.make_async_copy(g_hbm, g_ref, g_s),
    ]

    def x_load(i):
        return pltpu.make_async_copy(x_hbm.at[tile(i), :], x_ref.at[tile(i), :], x_s.at[i])

    for load in loads:
        load.start()
    for i in range(3):
        x_load(i).start()
    for load in late_loads:
        load.start()

    barrier = pltpu.get_barrier_semaphore()

    def greet(r, carry):
        pl.semaphore_signal(barrier, inc=1, device_id={"tensor": (t + r) % 16}, device_id_type=MESH)
        return carry

    lax.fori_loop(1, 16, greet, 0)
    for other in (left, right, y_partner) + tuple(z_peer(r) for r in Z_STEPS):
        pl.semaphore_signal(barrier, inc=1, device_id={"patch": other}, device_id_type=MESH)

    for load in loads:
        load.wait()
    for to, at, size in ((0, 64, 128), (128, 0, 64), (192, 192, 64)):
        wt[to : to + size, :] = (
            pw_ref[at : at + size, :].astype(F32) + wn_ref[at : at + size, :].astype(F32)
        ).astype(BF)

    gain = gain_ref[...]

    def halo_copy(side, i):
        return remote(
            kvw.at[1, tile(i), :], kvw.at[2 * side, tile(i), :],
            halo_s.at[side, i], halo_r.at[side, i], patch=left if side else right,
        )

    def project(i):
        rows = tile(i)
        x_load(i).wait()
        xs = x_ref[rows, :].astype(F32)
        inv = lax.rsqrt(jnp.sum(xs * xs, axis=1, keepdims=True) * (1.0 / D) + 1e-06)
        h = (xs * inv * gain).astype(BF)
        hid[rows, :] = h
        irms[rows, :] = jnp.broadcast_to(inv, (TILE, 128))
        pr = nt(h, wt[...])
        kvw[1, rows, :] = pr[:, :128].astype(BF)
        if i == 0:
            pl.semaphore_wait(barrier, 25)
        halo_copy(0, i).start()
        halo_copy(1, i).start()
        lane = lax.broadcasted_iota(jnp.int32, (TILE, 128), 1)
        q = jnp.where(lane < 64, pr[:, 128:].astype(BF).astype(F32), 0.0)
        qz[rows, :] = (q * 0.125).astype(BF)
        q_t[:, rows] = jnp.transpose(q)[:64, :].astype(BF)

    for i in range(3):
        project(i)

    lane12 = lax.broadcasted_iota(jnp.int32, (CAP, 128), 1)
    for load in late_loads:
        load.wait()
    nb = nb_ref[...]
    member = lane12 == 64 + nb[:, 0:1]
    for j in range(1, NB):
        member = member | (lane12 == 64 + nb[:, j : j + 1])
    member = jnp.where(member, 0.0, OFF)
    member = jnp.where(lane12 == 100, 1.0, jnp.where(lane12 > 100, 0.0, member))
    lane64 = lax.broadcasted_iota(jnp.int32, (PIX, 128), 1)
    for b, owner in enumerate((left, p, right)):
        valid = pltpu.roll(pv_ref[...], SLOTS - owner * CAP, 1)[:, :128]
        valid = jnp.where(valid > 0, 0.0, OFF)
        for s in range(CAP):
            aux = jnp.where(lane64 == 64 + b * CAP + s, 1.0, 0.0)
            aux = jnp.where(lane64 == 100, valid[:, s : s + 1], aux)
            kaug[b, s * PIX : (s + 1) * PIX, :] = aux.astype(BF)

    live = counts_ref[p] * PIX

    def upstream(i, carry):
        rows = tile(i)
        row = lax.broadcasted_iota(jnp.int32, (TILE, 1), 0) + i * TILE
        g = jnp.where(row < live, g_ref[rows, :].astype(F32), 0.0).astype(BF)
        up[rows, :] = g
        og = nt(g, wt[128:256, :])
        lane = lax.broadcasted_iota(jnp.int32, (TILE, 128), 1)
        dz[rows, :] = jnp.where(lane >= 64, og, 0.0).astype(BF)
        return carry

    lax.fori_loop(0, 3, upstream, 0)
    for s in range(CAP):
        rows = slice(s * PIX, (s + 1) * PIX)
        qaug[rows, :] = jnp.where(lane64 < 64, qz[rows, :].astype(F32), member[s : s + 1, :]).astype(BF)

    def fold(value, op):
        return op(value.reshape(value.shape[0] // 8, 8, value.shape[1]), axis=0)

    def score(b):
        base = b * ROWS
        for i in range(3):
            rows = tile(i)
            kv = kvw[b, rows, :].astype(F32)
            lane = lax.broadcasted_iota(jnp.int32, (TILE, 128), 1)
            kaug[b, rows, :] = jnp.where(lane < 64, kv, kaug[b, rows, :].astype(F32)).astype(BF)
            kvt[b, :, rows] = jnp.transpose(kv).astype(BF)
        for q in range(3):
            cols = tile(q)
            s = nt(kaug[b], qaug[cols, :])
            sc[base : base + ROWS, cols] = s
            mx[b, :, cols] = fold(s, jnp.max)
            dp[base : base + ROWS, cols] = nt(kvw[b], dz[cols, :])

    def raise_block(b, q, top):
        cols = tile(q)
        total = jnp.zeros((8, TILE), F32)
        weighted = jnp.zeros((8, TILE), F32)
        for i in range(3):
            rows = tile(b * 3 + i)
            e = jnp.exp(sc[rows, cols] - top)
            sc[rows, cols] = e
            total = total + fold(e, jnp.sum)
            weighted = weighted + fold(e * dp[rows, cols], jnp.sum)
        return total, weighted

    def divide_block(b, q, inv, delta):
        cols = tile(q)
        for i in range(3):
            rows = tile(b * 3 + i)
            att = sc[rows, cols] * inv
            pt[rows, cols] = att.astype(BF)
            ds_t[rows, cols] = (att * (dp[rows, cols] - delta)).astype(BF)

    score(1)
    for q in range(3):
        cols = tile(q)
        top = jnp.max(mx[1, :, cols], axis=0, keepdims=True)
        sums[0, :, cols], sums[1, :, cols] = raise_block(1, q, top)

    odd = core == 1
    share = pl.ds(pl.multiple_of((t // 2) * 128, 128), 128)

    def mine(value):
        turned = jnp.transpose(value)
        return jnp.where(odd, turned[64:, :], turned[:64, :])

    gain_share = mine(jnp.broadcast_to(gain_ref[:, share], (128, 128)))[:, :1]

    def shares(i, carry):
        rows = tile(i)
        inv = jnp.transpose(irms[rows, :])[:1, :]
        fscale[:, rows] = gain_share * inv
        nshare[:, rows] = mine(x_ref[rows, share].astype(F32)) * (inv * inv)
        ushare[:, rows] = mine(up[rows, share].astype(F32))
        return carry

    lax.fori_loop(0, 3, shares, 0)

    order = [(2, 0), (2, 1), (1, 0), (3, 0), (0, 0), (1, 1), (3, 1), (0, 1)]

    def block_of(o):
        dx, k = order[o]
        y = (1 - y_hi) if k == 0 else y_hi
        return y * NX + (x + dx) % NX

    for o in range(8):
        wk[o * 128 : (o + 1) * 128, :] = jnp.transpose(wt[:, tile(block_of(o), 128)].astype(F32)).astype(BF)

    for side in range(2):
        for i in range(3):
            halo_copy(side, i).wait_recv()
        score(2 * side)

    def row(value):
        return jnp.max(value, axis=0, keepdims=True)

    own_scale = []
    for q in range(3):
        cols = tile(q)
        own_top = row(mx[1, :, cols])
        top = jnp.maximum(own_top, jnp.maximum(row(mx[0, :, cols]), row(mx[2, :, cols])))
        shrink = jnp.exp(own_top - top)
        total, weighted = sums[0, :, cols] * shrink, sums[1, :, cols] * shrink
        for b in (0, 2):
            part_total, part_weighted = raise_block(b, q, top)
            total, weighted = total + part_total, weighted + part_weighted
        inv = 1.0 / jnp.sum(total, axis=0, keepdims=True)
        delta = jnp.sum(weighted, axis=0, keepdims=True) * inv
        for b in (0, 2):
            divide_block(b, q, inv, delta)
        own_scale.append((inv * shrink, delta))

    def near_grad(start, size):
        at = pl.ds(start, size)
        return nn(ds_t[at, :], qz[...]) + nn(pt[at, :], dz[...])

    def grad_copy(side, i):
        rows = pl.ds(i * HALF, HALF)
        return remote(
            halo_out.at[side, rows, :], halo_in.at[1 - side, rows, :],
            hg_s.at[side, i], hg_r.at[1 - side, i], patch=right if side else left,
        )

    for i in range(2):
        for side in range(2):
            rows = pl.ds(i * HALF, HALF)
            halo_out[side, rows, :] = near_grad(2 * side * ROWS + i * HALF, HALF).astype(BF)
            grad_copy(side, i).start()

    for q in range(3):
        divide_block(1, q, *own_scale[q])
    own_grad[...] = near_grad(ROWS, ROWS)

    def query_side(q, carry):
        cols = tile(q)
        qg = jnp.zeros((64, TILE), F32)
        at = jnp.zeros((64, TILE), F32)
        for b in range(3):
            rows = slice(b * ROWS, (b + 1) * ROWS)
            qg = qg + nn(kvt[b, 0:64, :], ds_t[rows, cols])
            at = at + nn(kvt[b, 64:128, :], pt[rows, cols])
        grads_t[128:192, cols] = (qg * 0.125).astype(BF)
        att_t[:, cols] = at.astype(BF)
        return carry

    for q in range(3):
        query_side(q, 0)

    def weight_qo(n, carry):
        cols = tile(n)
        both = jnp.concatenate(
            [nn(grads_t[128:192, :], hid[:, cols]), nn(att_t[...], up[:, cols])], axis=0
        )
        pj[0, cols, :] = jnp.transpose(both).astype(BF)
        return carry

    for n in range(4):
        weight_qo(n, 0)

    def y_copy(h):
        return remote(
            pj.at[h, tile(1 - y_lo, 512), :], y_in.at[h], y_s.at[h], y_r.at[h], patch=y_partner
        )

    y_copy(0).start()

    for i in range(2):
        for side in range(2):
            grad_copy(side, i).wait_recv()

    def collect(i, carry):
        rows = tile(i)
        total = (
            own_grad[rows, :] + halo_in[0, rows, :].astype(F32) + halo_in[1, rows, :].astype(F32)
        )
        kvg = jnp.transpose(total).astype(BF)
        grads_t[0:128, rows] = kvg
        prod = jnp.sum(kvg.astype(F32) * kvt[1, :, rows].astype(F32), axis=0, keepdims=True)
        qg = grads_t[128:192, rows].astype(F32) * q_t[:, rows].astype(F32)
        prod = prod + jnp.sum(qg, axis=0, keepdims=True)
        for j in range(2):
            m_out[pl.ds(2 * i + j, 1), :] = prod[:, j * 128 : (j + 1) * 128]
        return carry

    m_out[...] = jnp.zeros_like(m_out)
    for i in range(3):
        collect(i, 0)

    def core_copy(o):
        return remote(
            part.at[o, tile(1 - core, 64), :], r1.at[o], c_s.at[o], c_r.at[o], tensor=core_partner
        )

    for group in range(2):
        some = nn(wk[group * 512 : (group + 1) * 512, 0:192], grads_t[...])
        for n in range(4):
            o = group * 4 + n
            part[o] = some[n * 128 : (n + 1) * 128, :].astype(BF)
            core_copy(o).start()

    def m_send(r, carry):
        remote(m_out, m_in.at[r - 1], m_s, m_r, tensor=(t + r) % 16).start()
        return carry

    lax.fori_loop(1, 16, m_send, 0)

    def pair_sum(o):
        core_copy(o).wait_recv()
        return part[o, tile(core, 64), :].astype(F32) + r1[o].astype(F32)

    def r2_copy(k, side):
        half = slice(side * 32, side * 32 + 32)
        return remote(
            s2.at[k, half, :], r2.at[side, k], r2_s.at[side, k], r2_r.at[side, k],
            tensor=x_right if side == 0 else x_left,
        )

    def r3_copy(k, side, half):
        o = 2 + 3 * k + side
        rows = slice(half * 32, half * 32 + 32)
        return remote(
            s2.at[o, rows, :], r3.at[side, k, rows, :], r3_s.at[side, k, half], r3_r.at[side, k, half],
            tensor=x_right if side == 0 else x_left,
        )

    def a_copy(h, n):
        step = (1, 15, 2, 14)[n]
        rows = (slice(0, 128), slice(0, 128), slice(0, 64), slice(64, 128))[n]
        return remote(
            z_out.at[h, (z + step) % 4, rows, :], z_in.at[h, n, rows, :],
            za_s.at[h, n], za_r.at[h, n], patch=z_peer(step),
        )

    def b_copy(h, r):
        return remote(
            zb_out.at[h, tile((z // 4 + r) % 4, 32), :], zb_in.at[h, r - 1],
            zb_s.at[h, r - 1], zb_r.at[h, r - 1], patch=z_peer(4 * r),
        )

    def a_stage(h):
        y_copy(h).wait_recv()
        for d in range(Z):
            rows = pl.ds(pl.multiple_of(y_lo * 512 + d * 32, 32), 32)
            both = pj[h, rows, :].astype(F32) + y_in[h, d * 32 : d * 32 + 32, :].astype(F32)
            z_out[h, d % 4, (d // 4) * 32 : (d // 4) * 32 + 32, :] = both.astype(BF)
        for n in range(4):
            a_copy(h, n).start()

    def b_stage(h):
        for n in range(4):
            a_copy(h, n).wait_recv()
        for i in range(2):
            rows = slice(i * 64, i * 64 + 64)
            total = z_out[h, z % 4, rows, :].astype(F32)
            for n in (0, 1, 2 + i):
                total = total + z_in[h, n, rows, :].astype(F32)
            zb_out[h, rows, :] = total.astype(BF)
        for r in range(1, 4):
            b_copy(h, r).start()

    def z_total(h):
        total = zb_out[h, tile(z // 4, 32), :].astype(F32)
        for r in range(1, 4):
            b_copy(h, r).wait_recv()
            total = total + zb_in[h, r - 1].astype(F32)
        for half in range(2):
            pg_ref[:, (1, 2)[half] if h else (0, 3)[half], :] = total[:, half * 64 : half * 64 + 64]

    for k in range(2):
        s2[k] = pair_sum(k).astype(BF)
        for side in range(2):
            r2_copy(k, side).start()
    for k in range(2):
        for side in range(2):
            o = 2 + 3 * k + side
            s2[o] = pair_sum(o).astype(BF)
            r3_copy(k, side, 1 - side).start()
    a_stage(0)

    for n in range(4):
        cols = tile(n)
        pj[1, cols, :] = jnp.transpose(nn(grads_t[0:128, :], hid[:, cols])).astype(BF)
    y_copy(1).start()

    for k in range(2):
        for side in range(2):
            o = 2 + 3 * k + side
            half = slice(side * 32, side * 32 + 32)
            r2_copy(k, side).wait_recv()
            s2[o, half, :] = (
                pair_sum_again(part, r1, core, o, half) + r2[side, k].astype(F32)
            ).astype(BF)
            r3_copy(k, side, side).start()
    b_stage(0)
    a_stage(1)

    def x_sum(k):
        o = 4 + 3 * k
        total = pair_sum(o)
        for side in range(2):
            for half in range(2):
                r3_copy(k, side, half).wait_recv()
            total = total + r3[side, k].astype(F32)
        return total

    r4_copy = remote(s3, r4, r4_s, r4_r, tensor=hi_partner)
    s3[...] = x_sum(0).astype(BF)
    r4_copy.start()
    b_stage(1)
    z_total(0)
    feature = x_sum(1)
    z_total(1)

    pltpu.make_async_copy(m_in, m_in, m_r).wait()
    m = m_out[...]
    for r in range(15):
        m = m + m_in[r]
    m = m * (1.0 / D)
    mean = jnp.concatenate([m[i : i + 1, :] for i in range(6)], axis=1)

    r4_copy.wait_recv()
    feature = feature + r4[...].astype(F32)
    og_ref[...] = (ushare[...] + feature * fscale[...] - nshare[...] * mean).astype(BF)

    for side in range(2):
        for i in range(3):
            halo_copy(side, i).wait_send()
        for i in range(2):
            grad_copy(side, i).wait_send()
    for o in range(8):
        core_copy(o).wait_send()
    for k in range(2):
        for side in range(2):
            r2_copy(k, side).wait_send()
            for half in range(2):
                r3_copy(k, side, half).wait_send()
    r4_copy.wait_send()
    for h in range(2):
        y_copy(h).wait_send()
        for n in range(4):
            a_copy(h, n).wait_send()
        for r in range(1, 4):
            b_copy(h, r).wait_send()
    pltpu.make_async_copy(m_in, m_in, m_s).wait()


def pair_sum_again(part, r1, core, o, half):
    rows = pl.ds(pl.multiple_of(core * 64 + half.start, 32), 32)
    return part[o, rows, :].astype(F32) + r1[o, half, :].astype(F32)


def per_device(
    inputs, cotangent, norm_gain, proj_weight, weight_noise, patch_counts, neighbours, pixel_valid
):
    def turned(weight):
        return jnp.transpose(weight, (1, 2, 0)).reshape(4 * weight.shape[2], D)

    vmem = pl.BlockSpec(memory_space=pltpu.VMEM)
    smem = pl.BlockSpec(memory_space=pltpu.SMEM)
    hbm = pl.BlockSpec(memory_space=pl.ANY)
    V = pltpu.VMEM
    dma = pltpu.SemaphoreType.DMA
    grad, proj = pl.pallas_call(
        kernel,
        out_shape=(
            jax.ShapeDtypeStruct((64, ROWS), BF),
            jax.ShapeDtypeStruct((32, 4, 64), F32),
        ),
        in_specs=[hbm, hbm, hbm, hbm, hbm, smem, hbm, hbm],
        out_specs=(vmem, vmem),
        scratch_shapes=[
            V((ROWS, D), BF),
            V((ROWS, D), BF),
            V((1, D), F32),
            V((256, D), BF),
            V((256, D), BF),
            V((CAP, NB), jnp.int32),
            V((PIX, SLOTS), jnp.int32),
            V((256, D), BF),
            V((D, 256), BF),
            V((ROWS, D), BF),
            V((ROWS, D), BF),
            V((ROWS, 128), F32),
            V((64, ROWS), F32),
            V((64, ROWS), F32),
            V((64, ROWS), F32),
            V((3, ROWS, 128), BF),
            V((3, 128, ROWS), BF),
            V((3, ROWS, 128), BF),
            V((ROWS, 128), BF),
            V((ROWS, 128), BF),
            V((ROWS, 128), BF),
            V((64, ROWS), BF),
            V((3 * ROWS, ROWS), F32),
            V((3 * ROWS, ROWS), F32),
            V((3, 8, ROWS), F32),
            V((2, 8, ROWS), F32),
            V((3 * ROWS, ROWS), BF),
            V((3 * ROWS, ROWS), BF),
            V((2, ROWS, 128), BF),
            V((ROWS, 128), F32),
            V((2, ROWS, 128), BF),
            V((64, ROWS), BF),
            V((192, ROWS), BF),
            V((8, 128), F32),
            V((15, 8, 128), F32),
            V((2, D, 128), BF),
            V((2, 512, 128), BF),
            V((2, 4, 128, 128), BF),
            V((2, 4, 128, 128), BF),
            V((2, 128, 128), BF),
            V((2, 3, 32, 128), BF),
            V((8, 128, ROWS), BF),
            V((8, 64, ROWS), BF),
            V((8, 64, ROWS), BF),
            V((2, 2, 32, ROWS), BF),
            V((2, 2, 64, ROWS), BF),
            V((64, ROWS), BF),
            V((64, ROWS), BF),
            dma((3,)), dma, dma((5,)),
            dma((2, 3)), dma((2, 3)),
            dma((2, 2)), dma((2, 2)),
            dma, dma,
            dma((2,)), dma((2,)),
            dma((2, 4)), dma((2, 4)),
            dma((2, 3)), dma((2, 3)),
            dma((8,)), dma((8,)),
            dma((2, 2)), dma((2, 2)),
            dma((2, 2, 2)), dma((2, 2, 2)),
            dma, dma,
        ],
        compiler_params=pltpu.CompilerParams(
            collective_id=0, has_side_effects=True, vmem_limit_bytes=56 * 1024 * 1024
        ),
        cost_estimate=pl.CostEstimate(
            flops=4 * 10**9, bytes_accessed=5 * 10**6, transcendentals=2 * 10**6
        ),
    )(
        inputs,
        cotangent,
        norm_gain.reshape(1, D),
        turned(proj_weight),
        turned(weight_noise),
        patch_counts,
        neighbours,
        jnp.transpose(pixel_valid),
    )
    return (jnp.transpose(grad), proj)


def solution(mesh):
    placed = (
        P("patch", None),
        P("patch", None),
        P(),
        P(None, None, "tensor"),
        P(None, None, "tensor"),
        P(),
        P("patch", None),
        P(),
    )
    return jax.shard_map(
        per_device,
        mesh=mesh,
        in_specs=placed,
        out_specs=(P("patch", "tensor"), P("patch", None, "tensor")),
        check_vma=False,
    )
```

```python
import jax
import jax.numpy as jnp
from jax import lax
from jax.experimental import pallas as pl
from jax.experimental.pallas import tpu as pltpu
from jax.sharding import PartitionSpec as P

BF = jnp.bfloat16
F32 = jnp.float32
MESH = pl.DeviceIdType.MESH
OFF = -1e30

ROWS = 768
D = 1024
PIX = 64
CAP = 12
NB = 9
TILE = 256
Z = 16
SLOTS = 384
NX = 4


def nn(a, b):
    return lax.dot_general(a, b, (((1,), (0,)), ((), ())), preferred_element_type=F32)


def nt(a, b):
    return lax.dot_general(a, b, (((1,), (1,)), ((), ())), preferred_element_type=F32)


def tile(i, size=TILE):
    if isinstance(i, int):
        return pl.ds(i * size, size)
    return pl.ds(pl.multiple_of(i * size, size), size)


def remote(src, dst, send_sem, recv_sem, **device):
    return pltpu.make_async_remote_copy(
        src_ref=src,
        dst_ref=dst,
        send_sem=send_sem,
        recv_sem=recv_sem,
        device_id=device,
        device_id_type=MESH,
    )


def kernel(
    x_hbm, g_hbm, gain_hbm, pw_hbm, wn_hbm, counts_hbm, nb_hbm, pv_hbm,
    og_ref, pg_ref,
    x_ref, g_ref, gain_ref, pw_ref, wn_ref, counts_ref, nb_ref, pv_ref, wt, wk, hid, up, irms, fscale, nshare, ushare, kvw, kvt, kaug, qaug, qz, dz, q_t,
    sc, dp, mx, sums, pt, ds_t, halo_out, own_grad, halo_in, att_t, grads_t,
    m_out, m_in, pj, a_in, b_out, b_in,
    part, r1, s2, r2,
    x_s, g_s, w_s, halo_s, halo_r, hg_s, hg_r, m_s, m_r, a_s, a_r, b_s, b_r,
    c_s, c_r, r2_s, r2_r, known,
):
    p = lax.axis_index("patch")
    t = lax.axis_index("tensor")
    y_lo, z = p // Z, p % Z
    core = t % 2
    x = (t // 2) % NX
    y_hi = t // 8
    right, left = (p + 1) % 32, (p + 31) % 32
    core_partner = t + 1 - 2 * core

    def z_peer(r, other=0):
        return (1 - y_lo if other else y_lo) * Z + (z + r) % Z

    loads = [
        pltpu.make_async_copy(pw_hbm, pw_ref, w_s.at[0]),
        pltpu.make_async_copy(wn_hbm, wn_ref, w_s.at[1]),
        pltpu.make_async_copy(gain_hbm, gain_ref, w_s.at[2]),
    ]
    late_loads = [
        pltpu.make_async_copy(counts_hbm, counts_ref, w_s.at[5]),
        pltpu.make_async_copy(nb_hbm, nb_ref, w_s.at[3]),
        pltpu.make_async_copy(pv_hbm, pv_ref, w_s.at[4]),
        pltpu.make_async_copy(g_hbm, g_ref, g_s),
    ]

    def x_load(i):
        return pltpu.make_async_copy(x_hbm.at[tile(i), :], x_ref.at[tile(i), :], x_s.at[i])

    for load in loads:
        load.start()
    for i in range(3):
        x_load(i).start()
    for load in late_loads:
        load.start()

    barrier = pltpu.get_barrier_semaphore()

    def patch_of(r, other=0):
        return {"patch": z_peer(r, other)}

    row0 = t - x * 2
    near = [
        {"patch": left}, {"patch": right}, {"tensor": core_partner},
        {"tensor": row0 + (x + 1) % NX * 2}, {"tensor": row0 + (x + 3) % NX * 2},
        {"tensor": (t + 8) % 16}, patch_of(0, 1), patch_of(1), patch_of(15),
    ]
    rounds = [near, near + [patch_of(2), patch_of(14)], [near[2], patch_of(4), patch_of(12)]]

    def tell(semaphore, partners):
        for device in partners:
            pl.semaphore_signal(semaphore, inc=1, device_id=device, device_id_type=MESH)

    def tell_round(n):
        tell(known.at[n], rounds[n])

    def hear_round(n):
        pl.semaphore_wait(known.at[n], len(rounds[n]))

    tell(barrier, near)

    for load in loads:
        load.wait()
    for to, at, size in ((0, 64, 128), (128, 0, 64), (192, 192, 64)):
        wt[to : to + size, :] = (
            pw_ref[at : at + size, :].astype(F32) + wn_ref[at : at + size, :].astype(F32)
        ).astype(BF)

    gain = gain_ref[...]

    def halo_copy(side, i):
        return remote(
            kvw.at[1, tile(i), :], kvw.at[2 * side, tile(i), :],
            halo_s.at[side, i], halo_r.at[side, i], patch=left if side else right,
        )

    def project(i):
        rows = tile(i)
        x_load(i).wait()
        xs = x_ref[rows, :].astype(F32)
        inv = lax.rsqrt(jnp.sum(xs * xs, axis=1, keepdims=True) * (1.0 / D) + 1e-06)
        h = (xs * inv * gain).astype(BF)
        hid[rows, :] = h
        irms[rows, :] = jnp.broadcast_to(inv, (TILE, 128))
        pr = nt(h, wt[...])
        kvw[1, rows, :] = pr[:, :128].astype(BF)
        if i == 0:
            pl.semaphore_wait(barrier, len(near))
            tell_round(0)
        halo_copy(0, i).start()
        halo_copy(1, i).start()
        lane = lax.broadcasted_iota(jnp.int32, (TILE, 128), 1)
        q = jnp.where(lane < 64, pr[:, 128:].astype(BF).astype(F32), 0.0)
        qz[rows, :] = (q * 0.125).astype(BF)
        q_t[:, rows] = jnp.transpose(q)[:64, :].astype(BF)

    for i in range(3):
        project(i)

    lane12 = lax.broadcasted_iota(jnp.int32, (CAP, 128), 1)
    for load in late_loads:
        load.wait()
    nb = nb_ref[...]
    member = lane12 == 64 + nb[:, 0:1]
    for j in range(1, NB):
        member = member | (lane12 == 64 + nb[:, j : j + 1])
    member = jnp.where(member, 0.0, OFF)
    member = jnp.where(lane12 == 100, 1.0, jnp.where(lane12 > 100, 0.0, member))
    lane64 = lax.broadcasted_iota(jnp.int32, (PIX, 128), 1)
    for b, owner in enumerate((left, p, right)):
        valid = pltpu.roll(pv_ref[...], SLOTS - owner * CAP, 1)[:, :128]
        valid = jnp.where(valid > 0, 0.0, OFF)
        for s in range(CAP):
            aux = jnp.where(lane64 == 64 + b * CAP + s, 1.0, 0.0)
            aux = jnp.where(lane64 == 100, valid[:, s : s + 1], aux)
            kaug[b, s * PIX : (s + 1) * PIX, :] = aux.astype(BF)

    live = counts_ref[p] * PIX

    def upstream(i, carry):
        rows = tile(i)
        row = lax.broadcasted_iota(jnp.int32, (TILE, 1), 0) + i * TILE
        g = jnp.where(row < live, g_ref[rows, :].astype(F32), 0.0).astype(BF)
        up[rows, :] = g
        og = nt(g, wt[128:256, :])
        lane = lax.broadcasted_iota(jnp.int32, (TILE, 128), 1)
        dz[rows, :] = jnp.where(lane >= 64, og, 0.0).astype(BF)
        return carry

    lax.fori_loop(0, 3, upstream, 0)
    for s in range(CAP):
        rows = slice(s * PIX, (s + 1) * PIX)
        qaug[rows, :] = jnp.where(lane64 < 64, qz[rows, :].astype(F32), member[s : s + 1, :]).astype(BF)

    def fold(value, op):
        return op(value.reshape(value.shape[0] // 8, 8, value.shape[1]), axis=0)

    def score(b, i):
        rows = tile(i)
        at = tile(b * 3 + i)
        kv = kvw[b, rows, :].astype(F32)
        lane = lax.broadcasted_iota(jnp.int32, (TILE, 128), 1)
        kaug[b, rows, :] = jnp.where(lane < 64, kv, kaug[b, rows, :].astype(F32)).astype(BF)
        kvt[b, :, rows] = jnp.transpose(kv).astype(BF)
        for q in range(3):
            cols = tile(q)
            s = nt(kaug[b, rows, :], qaug[cols, :])
            sc[at, cols] = s
            mx[b * 3 + i, :, cols] = fold(s, jnp.max)
            dp[at, cols] = nt(kvw[b, rows, :], dz[cols, :])

    def top_of(b, cols):
        return jnp.max(jnp.max(mx[b * 3 : b * 3 + 3, :, cols], axis=0), axis=0, keepdims=True)

    def raise_block(b, q, top):
        cols = tile(q)
        total = jnp.zeros((8, TILE), F32)
        weighted = jnp.zeros((8, TILE), F32)
        for i in range(3):
            rows = tile(b * 3 + i)
            e = jnp.exp(sc[rows, cols] - top)
            sc[rows, cols] = e
            total = total + fold(e, jnp.sum)
            weighted = weighted + fold(e * dp[rows, cols], jnp.sum)
        return total, weighted

    def divide_block(b, q, inv, delta):
        cols = tile(q)
        for i in range(3):
            rows = tile(b * 3 + i)
            att = sc[rows, cols] * inv
            pt[rows, cols] = att.astype(BF)
            ds_t[rows, cols] = (att * (dp[rows, cols] - delta)).astype(BF)

    hear_round(0)
    tell_round(1)

    for i in range(3):
        score(1, i)
    for q in range(3):
        cols = tile(q)
        sums[0, :, cols], sums[1, :, cols] = raise_block(1, q, top_of(1, cols))

    for i in range(3):
        for side in range(2):
            halo_copy(side, i).wait_recv()
            score(2 * side, i)

    scales = []
    for q in range(3):
        cols = tile(q)
        own_top = top_of(1, cols)
        top = jnp.maximum(own_top, jnp.maximum(top_of(0, cols), top_of(2, cols)))
        shrink = jnp.exp(own_top - top)
        total, weighted = sums[0, :, cols] * shrink, sums[1, :, cols] * shrink
        for b in (0, 2):
            part_total, part_weighted = raise_block(b, q, top)
            total, weighted = total + part_total, weighted + part_weighted
        inv = 1.0 / jnp.sum(total, axis=0, keepdims=True)
        delta = jnp.sum(weighted, axis=0, keepdims=True) * inv
        scales.append((inv, inv * shrink, delta))

    def near_grad(b):
        at = tile(b, ROWS)
        return nn(ds_t[at, :], qz[...]) + nn(pt[at, :], dz[...])

    def grad_copy(side):
        return remote(
            halo_out.at[side], halo_in.at[1 - side], hg_s.at[side], hg_r.at[1 - side],
            patch=right if side else left,
        )

    for side in range(2):
        for q in range(3):
            divide_block(2 * side, q, scales[q][0], scales[q][2])
        halo_out[side] = near_grad(2 * side).astype(BF)
        grad_copy(side).start()

    for q in range(3):
        divide_block(1, q, scales[q][1], scales[q][2])
    own_grad[...] = near_grad(1)

    def query_side(q, carry):
        cols = tile(q)
        qg = jnp.zeros((64, TILE), F32)
        at = jnp.zeros((64, TILE), F32)
        for b in range(3):
            rows = slice(b * ROWS, (b + 1) * ROWS)
            qg = qg + nn(kvt[b, 0:64, :], ds_t[rows, cols])
            at = at + nn(kvt[b, 64:128, :], pt[rows, cols])
        grads_t[128:192, cols] = (qg * 0.125).astype(BF)
        att_t[:, cols] = at.astype(BF)
        return carry

    for q in range(3):
        query_side(q, 0)

    def put(h, n, value):
        for j in range(8):
            y, d = divmod(n * 8 + j, Z)
            pj[h, y, d % 4, (d // 4) * 32 : (d // 4) * 32 + 32, :] = value[j * 32 : j * 32 + 32, :]

    whole, first, last = slice(0, 128), slice(0, 64), slice(64, 128)
    window = [
        (1, 2, first), (1, 14, last), (0, 2, first), (0, 14, last),
        (1, 1, whole), (1, 15, whole), (1, 0, whole), (0, 1, whole), (0, 15, whole),
    ]

    def a_copy(h, n):
        other, step, rows = window[n]
        return remote(
            pj.at[h, 1 - y_lo if other else y_lo, (z + step) % 4, rows, :], a_in.at[h, n, rows, :],
            a_s.at[h, n], a_r.at[h, n], patch=z_peer(step, other),
        )

    def b_copy(h, r):
        return remote(
            b_out.at[h, tile((z // 4 + r) % 4, 32), :], b_in.at[h, r - 1],
            b_s.at[h, r - 1], b_r.at[h, r - 1], patch=z_peer(4 * r),
        )

    def a_stage(h):
        for n in range(9):
            a_copy(h, n).start()

    def b_stage(h):
        for n in range(9):
            a_copy(h, n).wait_recv()
        for i, rows in enumerate((first, last)):
            total = pj[h, y_lo, z % 4, rows, :].astype(F32)
            for n in (i, 2 + i, 4, 5, 6, 7, 8):
                total = total + a_in[h, n, rows, :].astype(F32)
            b_out[h, rows, :] = total.astype(BF)
        for r in (2, 1, 3):
            b_copy(h, r).start()

    def z_total(h):
        total = b_out[h, tile(z // 4, 32), :].astype(F32)
        for r in range(1, 4):
            b_copy(h, r).wait_recv()
            total = total + b_in[h, r - 1].astype(F32)
        for half in range(2):
            pg_ref[:, (1, 2)[half] if h else (0, 3)[half], :] = total[:, half * 64 : half * 64 + 64]

    for n in range(4):
        cols = tile(n)
        both = jnp.concatenate(
            [nn(grads_t[128:192, :], hid[:, cols]), nn(att_t[...], up[:, cols])], axis=0
        )
        put(0, n, jnp.transpose(both).astype(BF))
    hear_round(1)
    tell_round(2)
    a_stage(0)

    odd = core == 1
    share = pl.ds(pl.multiple_of((t // 2) * 128, 128), 128)

    def mine(value):
        turned = jnp.transpose(value)
        return jnp.where(odd, turned[64:, :], turned[:64, :])

    gain_share = mine(jnp.broadcast_to(gain_ref[:, share], (128, 128)))[:, :1]

    def shares(i, carry):
        rows = tile(i)
        inv = jnp.transpose(irms[rows, :])[:1, :]
        fscale[:, rows] = gain_share * inv
        nshare[:, rows] = mine(x_ref[rows, share].astype(F32)) * (inv * inv)
        ushare[:, rows] = mine(up[rows, share].astype(F32))
        return carry

    lax.fori_loop(0, 3, shares, 0)

    order = [(2, 0), (2, 1), (1, 0), (3, 0), (0, 0), (1, 1), (3, 1), (0, 1)]

    def block_of(o):
        dx, k = order[o]
        y = (1 - y_hi) if k == 0 else y_hi
        return y * NX + (x + dx) % NX

    for o in range(8):
        wk[o * 128 : (o + 1) * 128, :] = jnp.transpose(wt[:, tile(block_of(o), 128)].astype(F32)).astype(BF)

    for side in range(2):
        grad_copy(side).wait_recv()

    def collect(i, carry):
        rows = tile(i)
        total = (
            own_grad[rows, :] + halo_in[0, rows, :].astype(F32) + halo_in[1, rows, :].astype(F32)
        )
        kvg = jnp.transpose(total).astype(BF)
        grads_t[0:128, rows] = kvg
        prod = jnp.sum(kvg.astype(F32) * kvt[1, :, rows].astype(F32), axis=0, keepdims=True)
        qg = grads_t[128:192, rows].astype(F32) * q_t[:, rows].astype(F32)
        prod = prod + jnp.sum(qg, axis=0, keepdims=True)
        for j in range(2):
            m_out[pl.ds(2 * i + j, 1), :] = prod[:, j * 128 : (j + 1) * 128]
        return carry

    m_out[...] = jnp.zeros_like(m_out)
    for i in range(3):
        collect(i, 0)

    def core_copy(o):
        return remote(
            part.at[o, tile(1 - core, 64), :], r1.at[o], c_s.at[o], c_r.at[o], tensor=core_partner
        )

    def part_group(group):
        some = nn(wk[group * 512 : (group + 1) * 512, 0:192], grads_t[...])
        for n in range(4):
            o = group * 4 + n
            part[o] = some[n * 128 : (n + 1) * 128, :].astype(BF)
            core_copy(o).start()

    for n in range(4):
        put(1, n, jnp.transpose(nn(grads_t[0:128, :], hid[:, tile(n)])).astype(BF))
    a_stage(1)
    part_group(0)
    part_group(1)
    hear_round(2)

    def m_send(r, carry):
        remote(m_out, m_in.at[r - 1], m_s, m_r, tensor=(t + r) % 16).start()
        return carry

    lax.fori_loop(1, 16, m_send, 0)

    def pair_sum(o):
        core_copy(o).wait_recv()
        return part[o, tile(core, 64), :].astype(F32) + r1[o].astype(F32)

    def chip_copy(o):
        return remote(
            s2.at[o], r2.at[o], r2_s.at[o], r2_r.at[o], tensor=block_of(o) * 2 + core
        )

    for o in range(7):
        s2[o] = pair_sum(o).astype(BF)
        chip_copy(o).start()
    b_stage(0)
    feature = pair_sum(7)
    b_stage(1)
    z_total(0)

    pltpu.make_async_copy(m_in, m_in, m_r).wait()
    m = m_out[...]
    for r in range(15):
        m = m + m_in[r]
    m = m * (1.0 / D)
    mean = jnp.concatenate([m[i : i + 1, :] for i in range(6)], axis=1)

    for o in range(7):
        chip_copy(o).wait_recv()
        feature = feature + r2[o].astype(F32)
    og_ref[...] = (ushare[...] + feature * fscale[...] - nshare[...] * mean).astype(BF)
    z_total(1)

    for side in range(2):
        for i in range(3):
            halo_copy(side, i).wait_send()
        grad_copy(side).wait_send()
    for o in range(8):
        core_copy(o).wait_send()
    for o in range(7):
        chip_copy(o).wait_send()
    for h in range(2):
        for n in range(9):
            a_copy(h, n).wait_send()
        for r in range(1, 4):
            b_copy(h, r).wait_send()
    pltpu.make_async_copy(m_in, m_in, m_s).wait()


def per_device(
    inputs, cotangent, norm_gain, proj_weight, weight_noise, patch_counts, neighbours, pixel_valid
):
    def turned(weight):
        return jnp.transpose(weight, (1, 2, 0)).reshape(4 * weight.shape[2], D)

    vmem = pl.BlockSpec(memory_space=pltpu.VMEM)
    hbm = pl.BlockSpec(memory_space=pl.ANY)
    V = pltpu.VMEM
    dma = pltpu.SemaphoreType.DMA
    grad, proj = pl.pallas_call(
        kernel,
        out_shape=(
            jax.ShapeDtypeStruct((64, ROWS), BF),
            jax.ShapeDtypeStruct((32, 4, 64), F32),
        ),
        in_specs=[hbm] * 8,
        out_specs=(vmem, vmem),
        scratch_shapes=[
            V((ROWS, D), BF),
            V((ROWS, D), BF),
            V((1, D), F32),
            V((256, D), BF),
            V((256, D), BF),
            pltpu.SMEM((32,), jnp.int32),
            V((CAP, NB), jnp.int32),
            V((PIX, SLOTS), jnp.int32),
            V((256, D), BF),
            V((D, 256), BF),
            V((ROWS, D), BF),
            V((ROWS, D), BF),
            V((ROWS, 128), F32),
            V((64, ROWS), F32),
            V((64, ROWS), F32),
            V((64, ROWS), F32),
            V((3, ROWS, 128), BF),
            V((3, 128, ROWS), BF),
            V((3, ROWS, 128), BF),
            V((ROWS, 128), BF),
            V((ROWS, 128), BF),
            V((ROWS, 128), BF),
            V((64, ROWS), BF),
            V((3 * ROWS, ROWS), F32),
            V((3 * ROWS, ROWS), F32),
            V((9, 8, ROWS), F32),
            V((2, 8, ROWS), F32),
            V((3 * ROWS, ROWS), BF),
            V((3 * ROWS, ROWS), BF),
            V((2, ROWS, 128), BF),
            V((ROWS, 128), F32),
            V((2, ROWS, 128), BF),
            V((64, ROWS), BF),
            V((192, ROWS), BF),
            V((8, 128), F32),
            V((15, 8, 128), F32),
            V((2, 2, 4, 128, 128), BF),
            V((2, 9, 128, 128), BF),
            V((2, 128, 128), BF),
            V((2, 3, 32, 128), BF),
            V((8, 128, ROWS), BF),
            V((8, 64, ROWS), BF),
            V((7, 64, ROWS), BF),
            V((7, 64, ROWS), BF),
            dma((3,)), dma, dma((6,)),
            dma((2, 3)), dma((2, 3)),
            dma((2,)), dma((2,)),
            dma, dma,
            dma((2, 9)), dma((2, 9)),
            dma((2, 3)), dma((2, 3)),
            dma((8,)), dma((8,)),
            dma((7,)), dma((7,)),
            pltpu.SemaphoreType.REGULAR((3,)),
        ],
        compiler_params=pltpu.CompilerParams(
            collective_id=0, has_side_effects=True, vmem_limit_bytes=56 * 1024 * 1024
        ),
        cost_estimate=pl.CostEstimate(
            flops=4 * 10**9, bytes_accessed=5 * 10**6, transcendentals=2 * 10**6
        ),
    )(
        inputs,
        cotangent,
        norm_gain.reshape(1, D),
        turned(proj_weight),
        turned(weight_noise),
        patch_counts,
        neighbours,
        jnp.transpose(pixel_valid),
    )
    return (jnp.transpose(grad), proj)


def solution(mesh):
    placed = (
        P("patch", None),
        P("patch", None),
        P(),
        P(None, None, "tensor"),
        P(None, None, "tensor"),
        P(),
        P("patch", None),
        P(),
    )
    return jax.shard_map(
        per_device,
        mesh=mesh,
        in_specs=placed,
        out_specs=(P("patch", "tensor"), P("patch", None, "tensor")),
        check_vma=False,
    )
```

```python
import jax
import jax.numpy as jnp
from jax import lax
from jax.experimental import pallas as pl
from jax.experimental.pallas import tpu as pltpu
from jax.sharding import PartitionSpec as P

BF = jnp.bfloat16
F32 = jnp.float32
MESH = pl.DeviceIdType.MESH
OFF = -1e30

ROWS = 768
D = 1024
PIX = 64
CAP = 12
NB = 9
TILE = 256
Z = 16
SLOTS = 384
NX = 4


def nn(a, b):
    return lax.dot_general(a, b, (((1,), (0,)), ((), ())), preferred_element_type=F32)


def nt(a, b):
    return lax.dot_general(a, b, (((1,), (1,)), ((), ())), preferred_element_type=F32)


def tile(i, size=TILE):
    if isinstance(i, int):
        return pl.ds(i * size, size)
    return pl.ds(pl.multiple_of(i * size, size), size)


def remote(src, dst, send_sem, recv_sem, **device):
    return pltpu.make_async_remote_copy(
        src_ref=src,
        dst_ref=dst,
        send_sem=send_sem,
        recv_sem=recv_sem,
        device_id=device,
        device_id_type=MESH,
    )


def kernel(
    x_hbm, g_hbm, gain_hbm, pw_hbm, wn_hbm, counts_hbm, nb_hbm, pv_hbm,
    og_ref, pg_ref,
    x_ref, g_ref, gain_ref, pw_ref, wn_ref, counts_ref, nb_ref, pv_ref, wt, wk, hid, up, irms, fscale, nshare, ushare, kvw, kvt, kaug, qaug, q_raw, qz, dz, q_t,
    sc, dp, mx, sums, pt, ds_t, halo_out, own_grad, halo_in, att_t, grads_t,
    m_out, m_in, pj, a_in, b_out, b_in,
    part, r1, s2, r2,
    x_s, g_s, w_s, halo_s, halo_r, hg_s, hg_r, m_s, m_r, a_s, a_r, b_s, b_r,
    c_s, c_r, r2_s, r2_r, known,
):
    p = lax.axis_index("patch")
    t = lax.axis_index("tensor")
    y_lo, z = p // Z, p % Z
    core = t % 2
    x = (t // 2) % NX
    y_hi = t // 8
    right, left = (p + 1) % 32, (p + 31) % 32
    core_partner = t + 1 - 2 * core

    def z_peer(r, other=0):
        return (1 - y_lo if other else y_lo) * Z + (z + r) % Z

    loads = [
        pltpu.make_async_copy(gain_hbm, gain_ref, w_s.at[2]),
        pltpu.make_async_copy(pw_hbm, pw_ref, w_s.at[0]),
        pltpu.make_async_copy(wn_hbm, wn_ref, w_s.at[1]),
    ]
    late_loads = [
        pltpu.make_async_copy(counts_hbm, counts_ref, w_s.at[5]),
        pltpu.make_async_copy(nb_hbm, nb_ref, w_s.at[3]),
        pltpu.make_async_copy(pv_hbm, pv_ref, w_s.at[4]),
        pltpu.make_async_copy(g_hbm, g_ref, g_s),
    ]

    def x_load(i):
        return pltpu.make_async_copy(x_hbm.at[tile(i), :], x_ref.at[tile(i), :], x_s.at[i])

    x_load(0).start()
    for load in loads:
        load.start()
    for i in range(1, 3):
        x_load(i).start()
    for load in late_loads:
        load.start()

    barrier = pltpu.get_barrier_semaphore()

    def patch_of(r, other=0):
        return {"patch": z_peer(r, other)}

    row0 = t - x * 2
    near = [
        {"patch": left}, {"patch": right}, {"tensor": core_partner},
        {"tensor": row0 + (x + 1) % NX * 2}, {"tensor": row0 + (x + 3) % NX * 2},
        {"tensor": (t + 8) % 16}, patch_of(0, 1), patch_of(1), patch_of(15),
    ]
    rounds = [near, near + [patch_of(2), patch_of(14)], [near[2], patch_of(4), patch_of(12)]]

    def tell(semaphore, partners):
        for device in partners:
            pl.semaphore_signal(semaphore, inc=1, device_id=device, device_id_type=MESH)

    def tell_round(n):
        tell(known.at[n], rounds[n])

    def hear_round(n):
        pl.semaphore_wait(known.at[n], len(rounds[n]))

    tell(barrier, near)

    def norm(i):
        rows = tile(i)
        x_load(i).wait()
        xs = x_ref[rows, :].astype(F32)
        inv = lax.rsqrt(jnp.sum(xs * xs, axis=1, keepdims=True) * (1.0 / D) + 1e-06)
        hid[rows, :] = (xs * inv * gain_ref[...]).astype(BF)
        irms[rows, :] = jnp.broadcast_to(inv, (TILE, 128))

    loads[0].wait()
    norm(0)

    for load in loads[1:]:
        load.wait()
    for to, at, size in ((0, 64, 128), (128, 0, 64), (192, 192, 64)):
        wt[to : to + size, :] = (
            pw_ref[at : at + size, :].astype(F32) + wn_ref[at : at + size, :].astype(F32)
        ).astype(BF)

    def halo_copy(side, i):
        return remote(
            kvw.at[1, tile(i), :], kvw.at[2 * side, tile(i), :],
            halo_s.at[side, i], halo_r.at[side, i], patch=left if side else right,
        )

    for i in range(3):
        rows = tile(i)
        pr = nt(hid[rows, :], wt[...])
        if i < 2:
            norm(i + 1)
        kvw[1, rows, :] = pr[:, :128].astype(BF)
        q_raw[rows, :] = pr[:, 128:].astype(BF)
        if i == 0:
            pl.semaphore_wait(barrier, len(near))
        halo_copy(0, i).start()
        halo_copy(1, i).start()
    tell_round(0)

    def queries(i, carry):
        rows = tile(i)
        lane = lax.broadcasted_iota(jnp.int32, (TILE, 128), 1)
        q = jnp.where(lane < 64, q_raw[rows, :].astype(F32), 0.0)
        qz[rows, :] = (q * 0.125).astype(BF)
        q_t[:, rows] = jnp.transpose(q)[:64, :].astype(BF)
        return carry

    lax.fori_loop(0, 3, queries, 0)

    lane12 = lax.broadcasted_iota(jnp.int32, (CAP, 128), 1)
    for load in late_loads:
        load.wait()
    nb = nb_ref[...]
    member = lane12 == 64 + nb[:, 0:1]
    for j in range(1, NB):
        member = member | (lane12 == 64 + nb[:, j : j + 1])
    member = jnp.where(member, 0.0, OFF)
    member = jnp.where(lane12 == 100, 1.0, jnp.where(lane12 > 100, 0.0, member))
    lane64 = lax.broadcasted_iota(jnp.int32, (PIX, 128), 1)
    for b, owner in enumerate((left, p, right)):
        valid = pltpu.roll(pv_ref[...], SLOTS - owner * CAP, 1)[:, :128]
        valid = jnp.where(valid > 0, 0.0, OFF)
        for s in range(CAP):
            aux = jnp.where(lane64 == 64 + b * CAP + s, 1.0, 0.0)
            aux = jnp.where(lane64 == 100, valid[:, s : s + 1], aux)
            kaug[b, s * PIX : (s + 1) * PIX, :] = aux.astype(BF)

    live = counts_ref[p] * PIX

    def upstream(i, carry):
        rows = tile(i)
        row = lax.broadcasted_iota(jnp.int32, (TILE, 1), 0) + i * TILE
        g = jnp.where(row < live, g_ref[rows, :].astype(F32), 0.0).astype(BF)
        up[rows, :] = g
        og = nt(g, wt[128:256, :])
        lane = lax.broadcasted_iota(jnp.int32, (TILE, 128), 1)
        dz[rows, :] = jnp.where(lane >= 64, og, 0.0).astype(BF)
        return carry

    lax.fori_loop(0, 3, upstream, 0)
    for s in range(CAP):
        rows = slice(s * PIX, (s + 1) * PIX)
        qaug[rows, :] = jnp.where(lane64 < 64, qz[rows, :].astype(F32), member[s : s + 1, :]).astype(BF)

    def fold(value, op):
        return op(value.reshape(value.shape[0] // 8, 8, value.shape[1]), axis=0)

    def score(b, i):
        rows = tile(i)
        at = tile(b * 3 + i)
        kv = kvw[b, rows, :].astype(F32)
        lane = lax.broadcasted_iota(jnp.int32, (TILE, 128), 1)
        kaug[b, rows, :] = jnp.where(lane < 64, kv, kaug[b, rows, :].astype(F32)).astype(BF)
        kvt[b, :, rows] = jnp.transpose(kv).astype(BF)
        for q in range(3):
            cols = tile(q)
            s = nt(kaug[b, rows, :], qaug[cols, :])
            sc[at, cols] = s
            mx[b * 3 + i, :, cols] = fold(s, jnp.max)
            dp[at, cols] = nt(kvw[b, rows, :], dz[cols, :])

    def top_of(b, cols):
        return jnp.max(jnp.max(mx[b * 3 : b * 3 + 3, :, cols], axis=0), axis=0, keepdims=True)

    def raise_block(b, q, top):
        cols = tile(q)
        total = jnp.zeros((8, TILE), F32)
        weighted = jnp.zeros((8, TILE), F32)
        for i in range(3):
            rows = tile(b * 3 + i)
            e = jnp.exp(sc[rows, cols] - top)
            sc[rows, cols] = e
            total = total + fold(e, jnp.sum)
            weighted = weighted + fold(e * dp[rows, cols], jnp.sum)
        return total, weighted

    def divide_block(b, i, q, inv, delta):
        cols = tile(q)
        rows = tile(b * 3 + i)
        att = sc[rows, cols] * inv
        pt[rows, cols] = att.astype(BF)
        ds_t[rows, cols] = (att * (dp[rows, cols] - delta)).astype(BF)

    hear_round(0)
    tell_round(1)

    for i in range(3):
        score(1, i)
    for q in range(3):
        cols = tile(q)
        sums[0, :, cols], sums[1, :, cols] = raise_block(1, q, top_of(1, cols))

    for i in range(3):
        for side in range(2):
            halo_copy(side, i).wait_recv()
            score(2 * side, i)

    scales = []
    for q in range(3):
        cols = tile(q)
        own_top = top_of(1, cols)
        top = jnp.maximum(own_top, jnp.maximum(top_of(0, cols), top_of(2, cols)))
        shrink = jnp.exp(own_top - top)
        total, weighted = sums[0, :, cols] * shrink, sums[1, :, cols] * shrink
        for b in (0, 2):
            part_total, part_weighted = raise_block(b, q, top)
            total, weighted = total + part_total, weighted + part_weighted
        inv = 1.0 / jnp.sum(total, axis=0, keepdims=True)
        delta = jnp.sum(weighted, axis=0, keepdims=True) * inv
        scales.append((inv, inv * shrink, delta))

    def near_grad(start, size):
        at = pl.ds(start, size)
        return nn(ds_t[at, :], qz[...]) + nn(pt[at, :], dz[...])

    def grad_copy(side, i):
        return remote(
            halo_out.at[side, tile(i), :], halo_in.at[1 - side, tile(i), :],
            hg_s.at[side, i], hg_r.at[1 - side, i], patch=right if side else left,
        )

    chunks = [(side, i) for i in range(3) for side in range(2)]

    def divide_chunk(b, i, own):
        for q in range(3):
            divide_block(b, i, q, scales[q][own], scales[q][2])

    divide_chunk(0, 0, 0)
    for n, (side, i) in enumerate(chunks):
        grads = near_grad((2 * side * 3 + i) * TILE, TILE)
        if n + 1 < len(chunks):
            divide_chunk(2 * chunks[n + 1][0], chunks[n + 1][1], 0)
        halo_out[side, tile(i), :] = grads.astype(BF)
        grad_copy(side, i).start()

    for i in range(3):
        divide_chunk(1, i, 1)
    own_grad[...] = near_grad(ROWS, ROWS)

    def query_side(q, carry):
        cols = tile(q)
        qg = jnp.zeros((64, TILE), F32)
        at = jnp.zeros((64, TILE), F32)
        for b in range(3):
            rows = slice(b * ROWS, (b + 1) * ROWS)
            qg = qg + nn(kvt[b, 0:64, :], ds_t[rows, cols])
            at = at + nn(kvt[b, 64:128, :], pt[rows, cols])
        grads_t[128:192, cols] = (qg * 0.125).astype(BF)
        att_t[:, cols] = at.astype(BF)
        return carry

    for q in range(3):
        query_side(q, 0)

    def put(h, n, value):
        for j in range(8):
            y, d = divmod(n * 8 + j, Z)
            pj[h, y, d % 4, (d // 4) * 32 : (d // 4) * 32 + 32, :] = value[j * 32 : j * 32 + 32, :]

    whole, first, last = slice(0, 128), slice(0, 64), slice(64, 128)
    window = [
        (1, 2, first), (1, 14, last), (0, 2, first), (0, 14, last),
        (1, 1, whole), (1, 15, whole), (1, 0, whole), (0, 1, whole), (0, 15, whole),
    ]

    def a_copy(h, n):
        other, step, rows = window[n]
        return remote(
            pj.at[h, 1 - y_lo if other else y_lo, (z + step) % 4, rows, :], a_in.at[h, n, rows, :],
            a_s.at[h, n], a_r.at[h, n], patch=z_peer(step, other),
        )

    def b_copy(h, r):
        return remote(
            b_out.at[h, tile((z // 4 + r) % 4, 32), :], b_in.at[h, r - 1],
            b_s.at[h, r - 1], b_r.at[h, r - 1], patch=z_peer(4 * r),
        )

    def a_stage(h):
        for n in range(9):
            a_copy(h, n).start()

    def b_stage(h):
        for n in range(9):
            a_copy(h, n).wait_recv()
        for i, rows in enumerate((first, last)):
            total = pj[h, y_lo, z % 4, rows, :].astype(F32)
            for n in (i, 2 + i, 4, 5, 6, 7, 8):
                total = total + a_in[h, n, rows, :].astype(F32)
            b_out[h, rows, :] = total.astype(BF)
        for r in (2, 1, 3):
            b_copy(h, r).start()

    def z_total(h):
        total = b_out[h, tile(z // 4, 32), :].astype(F32)
        for r in range(1, 4):
            b_copy(h, r).wait_recv()
            total = total + b_in[h, r - 1].astype(F32)
        for half in range(2):
            pg_ref[:, (1, 2)[half] if h else (0, 3)[half], :] = total[:, half * 64 : half * 64 + 64]

    for n in range(4):
        cols = tile(n)
        both = jnp.concatenate(
            [nn(grads_t[128:192, :], hid[:, cols]), nn(att_t[...], up[:, cols])], axis=0
        )
        put(0, n, jnp.transpose(both).astype(BF))
    hear_round(1)
    tell_round(2)
    a_stage(0)

    odd = core == 1
    share = pl.ds(pl.multiple_of((t // 2) * 128, 128), 128)

    def mine(value):
        turned = jnp.transpose(value)
        return jnp.where(odd, turned[64:, :], turned[:64, :])

    gain_share = mine(jnp.broadcast_to(gain_ref[:, share], (128, 128)))[:, :1]

    def shares(i, carry):
        rows = tile(i)
        inv = jnp.transpose(irms[rows, :])[:1, :]
        fscale[:, rows] = gain_share * inv
        nshare[:, rows] = mine(x_ref[rows, share].astype(F32)) * (inv * inv)
        ushare[:, rows] = mine(up[rows, share].astype(F32))
        return carry

    lax.fori_loop(0, 3, shares, 0)

    order = [(2, 0), (1, 0), (3, 0), (2, 1), (1, 1), (3, 1), (0, 0), (0, 1)]

    def block_of(o):
        dx, k = order[o]
        y = (1 - y_hi) if k == 0 else y_hi
        return y * NX + (x + dx) % NX

    for o in range(8):
        wk[o * 128 : (o + 1) * 128, :] = jnp.transpose(wt[:, tile(block_of(o), 128)].astype(F32)).astype(BF)


    def collect(i):
        rows = tile(i)
        for side in range(2):
            grad_copy(side, i).wait_recv()
        total = (
            own_grad[rows, :] + halo_in[0, rows, :].astype(F32) + halo_in[1, rows, :].astype(F32)
        )
        kvg = jnp.transpose(total).astype(BF)
        grads_t[0:128, rows] = kvg
        prod = jnp.sum(kvg.astype(F32) * kvt[1, :, rows].astype(F32), axis=0, keepdims=True)
        qg = grads_t[128:192, rows].astype(F32) * q_t[:, rows].astype(F32)
        prod = prod + jnp.sum(qg, axis=0, keepdims=True)
        for j in range(2):
            m_out[pl.ds(2 * i + j, 1), :] = prod[:, j * 128 : (j + 1) * 128]

    m_out[...] = jnp.zeros_like(m_out)
    for i in range(3):
        collect(i)

    def core_copy(o):
        return remote(
            part.at[o, tile(1 - core, 64), :], r1.at[o], c_s.at[o], c_r.at[o], tensor=core_partner
        )

    def part_group(group):
        some = nn(wk[group * 512 : (group + 1) * 512, 0:192], grads_t[...])
        for n in range(4):
            o = group * 4 + n
            part[o] = some[n * 128 : (n + 1) * 128, :].astype(BF)
            core_copy(o).start()

    part_group(0)
    for n in range(4):
        put(1, n, jnp.transpose(nn(grads_t[0:128, :], hid[:, tile(n)])).astype(BF))
    a_stage(1)
    part_group(1)
    hear_round(2)

    def m_send(r, carry):
        remote(m_out, m_in.at[r - 1], m_s, m_r, tensor=(t + r) % 16).start()
        return carry

    lax.fori_loop(1, 16, m_send, 0)

    def pair_sum(o):
        core_copy(o).wait_recv()
        return part[o, tile(core, 64), :].astype(F32) + r1[o].astype(F32)

    def chip_copy(o):
        to = (t + 8) % 16 if o == 6 else row0 + (x + order[o][0]) % NX * 2
        return remote(s2.at[o], r2.at[o], r2_s.at[o], r2_r.at[o], tensor=to)

    def x_sum(k):
        total = pair_sum(6 + k)
        for o in range(3 * k, 3 * k + 3):
            chip_copy(o).wait_recv()
            total = total + r2[o].astype(F32)
        return total

    for o in range(6):
        s2[o] = pair_sum(o).astype(BF)
        chip_copy(o).start()
    b_stage(0)
    b_stage(1)
    s2[6] = x_sum(0).astype(BF)
    chip_copy(6).start()
    z_total(0)
    feature = x_sum(1)

    pltpu.make_async_copy(m_in, m_in, m_r).wait()
    m = m_out[...]
    for r in range(15):
        m = m + m_in[r]
    m = m * (1.0 / D)
    mean = jnp.concatenate([m[i : i + 1, :] for i in range(6)], axis=1)

    chip_copy(6).wait_recv()
    feature = feature + r2[6].astype(F32)
    og_ref[...] = (ushare[...] + feature * fscale[...] - nshare[...] * mean).astype(BF)
    z_total(1)

    for side in range(2):
        for i in range(3):
            halo_copy(side, i).wait_send()
            grad_copy(side, i).wait_send()
    for o in range(8):
        core_copy(o).wait_send()
    for o in range(7):
        chip_copy(o).wait_send()
    for h in range(2):
        for n in range(9):
            a_copy(h, n).wait_send()
        for r in range(1, 4):
            b_copy(h, r).wait_send()
    pltpu.make_async_copy(m_in, m_in, m_s).wait()


def per_device(
    inputs, cotangent, norm_gain, proj_weight, weight_noise, patch_counts, neighbours, pixel_valid
):
    def turned(weight):
        return jnp.transpose(weight, (1, 2, 0)).reshape(4 * weight.shape[2], D)

    vmem = pl.BlockSpec(memory_space=pltpu.VMEM)
    hbm = pl.BlockSpec(memory_space=pl.ANY)
    V = pltpu.VMEM
    dma = pltpu.SemaphoreType.DMA
    grad, proj = pl.pallas_call(
        kernel,
        out_shape=(V((64, ROWS), BF), V((32, 4, 64), F32)),
        in_specs=[hbm] * 8,
        out_specs=(vmem, vmem),
        scratch_shapes=[
            V((ROWS, D), BF),
            V((ROWS, D), BF),
            V((1, D), F32),
            V((256, D), BF),
            V((256, D), BF),
            pltpu.SMEM((32,), jnp.int32),
            V((CAP, NB), jnp.int32),
            V((PIX, SLOTS), jnp.int32),
            V((256, D), BF),
            V((D, 256), BF),
            V((ROWS, D), BF),
            V((ROWS, D), BF),
            V((ROWS, 128), F32),
            V((64, ROWS), F32),
            V((64, ROWS), F32),
            V((64, ROWS), F32),
            V((3, ROWS, 128), BF),
            V((3, 128, ROWS), BF),
            V((3, ROWS, 128), BF),
            V((ROWS, 128), BF),
            V((ROWS, 128), BF),
            V((ROWS, 128), BF),
            V((ROWS, 128), BF),
            V((64, ROWS), BF),
            V((3 * ROWS, ROWS), F32),
            V((3 * ROWS, ROWS), F32),
            V((9, 8, ROWS), F32),
            V((2, 8, ROWS), F32),
            V((3 * ROWS, ROWS), BF),
            V((3 * ROWS, ROWS), BF),
            V((2, ROWS, 128), BF),
            V((ROWS, 128), F32),
            V((2, ROWS, 128), BF),
            V((64, ROWS), BF),
            V((192, ROWS), BF),
            V((8, 128), F32),
            V((15, 8, 128), F32),
            V((2, 2, 4, 128, 128), BF),
            V((2, 9, 128, 128), BF),
            V((2, 128, 128), BF),
            V((2, 3, 32, 128), BF),
            V((8, 128, ROWS), BF),
            V((8, 64, ROWS), BF),
            V((7, 64, ROWS), BF),
            V((7, 64, ROWS), BF),
            dma((3,)), dma, dma((6,)),
            dma((2, 3)), dma((2, 3)),
            dma((2, 3)), dma((2, 3)),
            dma, dma,
            dma((2, 9)), dma((2, 9)),
            dma((2, 3)), dma((2, 3)),
            dma((8,)), dma((8,)),
            dma((7,)), dma((7,)),
            pltpu.SemaphoreType.REGULAR((3,)),
        ],
        compiler_params=pltpu.CompilerParams(
            collective_id=0, has_side_effects=True, vmem_limit_bytes=56 * 1024 * 1024
        ),
        cost_estimate=pl.CostEstimate(
            flops=4 * 10**9, bytes_accessed=5 * 10**6, transcendentals=2 * 10**6
        ),
    )(
        inputs,
        cotangent,
        norm_gain.reshape(1, D),
        turned(proj_weight),
        turned(weight_noise),
        patch_counts,
        neighbours,
        jnp.transpose(pixel_valid),
    )
    return (jnp.transpose(grad), proj)


def solution(mesh):
    placed = (
        P("patch", None),
        P("patch", None),
        P(),
        P(None, None, "tensor"),
        P(None, None, "tensor"),
        P(),
        P("patch", None),
        P(),
    )
    return jax.shard_map(
        per_device,
        mesh=mesh,
        in_specs=placed,
        out_specs=(P("patch", "tensor"), P("patch", None, "tensor")),
        check_vma=False,
    )
```

```python
import jax
import jax.numpy as jnp
from jax import lax
from jax.experimental import pallas as pl
from jax.experimental.pallas import tpu as pltpu
from jax.sharding import PartitionSpec as P

BF = jnp.bfloat16
F32 = jnp.float32
MESH = pl.DeviceIdType.MESH
OFF = -1e30

ROWS = 768
D = 1024
PIX = 64
CAP = 12
NB = 9
TILE = 256
Z = 16
SLOTS = 384
NX = 4


def nn(a, b):
    return lax.dot_general(a, b, (((1,), (0,)), ((), ())), preferred_element_type=F32)


def nt(a, b):
    return lax.dot_general(a, b, (((1,), (1,)), ((), ())), preferred_element_type=F32)


def tile(i, size=TILE):
    if isinstance(i, int):
        return pl.ds(i * size, size)
    return pl.ds(pl.multiple_of(i * size, size), size)


def remote(src, dst, send_sem, recv_sem, **device):
    return pltpu.make_async_remote_copy(
        src_ref=src,
        dst_ref=dst,
        send_sem=send_sem,
        recv_sem=recv_sem,
        device_id=device,
        device_id_type=MESH,
    )


def kernel(
    x_hbm, g_hbm, gain_hbm, pw_hbm, wn_hbm, counts_hbm, nb_hbm, pv_hbm,
    og_ref, pg_ref,
    x_ref, g_ref, gain_ref, pw_ref, wn_ref, counts_ref, nb_ref, pv_ref, wt, wk, hid, up, irms, fscale, nshare, ushare, kvw, kvt, kaug, qaug, q_raw, qz, dz, q_t,
    sc, dp, tops, sums, pt, ds_t, halo_out, own_grad, halo_in, att_t, grads_t,
    m_out, m_in, pj, a_in, b_out, b_in,
    part, r1, s2, r2, w_acc,
    x_s, g_s, w_s, halo_s, halo_r, hg_s, hg_r, m_s, m_r, a_s, a_r, b_s, b_r,
    c_s, c_r, r2_s, r2_r, known,
):
    p = lax.axis_index("patch")
    t = lax.axis_index("tensor")
    y_lo, z = p // Z, p % Z
    core = t % 2
    x = (t // 2) % NX
    y_hi = t // 8
    right, left = (p + 1) % 32, (p + 31) % 32
    core_partner = t + 1 - 2 * core

    def z_peer(r, other=0):
        return (1 - y_lo if other else y_lo) * Z + (z + r) % Z

    loads = [
        pltpu.make_async_copy(gain_hbm, gain_ref, w_s.at[2]),
        pltpu.make_async_copy(pw_hbm, pw_ref, w_s.at[0]),
        pltpu.make_async_copy(wn_hbm, wn_ref, w_s.at[1]),
    ]
    small_loads = [
        pltpu.make_async_copy(nb_hbm, nb_ref, w_s.at[3]),
        pltpu.make_async_copy(pv_hbm, pv_ref, w_s.at[4]),
    ]
    late_loads = [
        pltpu.make_async_copy(counts_hbm, counts_ref, w_s.at[5]),
        pltpu.make_async_copy(g_hbm, g_ref, g_s),
    ]

    def x_load(i):
        return pltpu.make_async_copy(x_hbm.at[tile(i), :], x_ref.at[tile(i), :], x_s.at[i])

    x_load(0).start()
    for load in loads:
        load.start()
    for i in range(1, 3):
        x_load(i).start()
    for load in small_loads + late_loads:
        load.start()

    barrier = pltpu.get_barrier_semaphore()

    def patch_of(r, other=0):
        return {"patch": z_peer(r, other)}

    row0 = t - x * 2
    near = [
        {"tensor": core_partner},
        {"tensor": row0 + (x + 1) % NX * 2}, {"tensor": row0 + (x + 3) % NX * 2},
        {"tensor": (t + 8) % 16}, patch_of(0, 1),
    ]
    beside = [patch_of(1), patch_of(15)]
    far = [[], beside, [near[0], patch_of(2), patch_of(14)], [patch_of(4), patch_of(12)]]
    has_left, has_right = p > 0, p < 31
    near_count = 5 + jnp.where(has_left, 1, 0) + jnp.where(has_right, 1, 0)

    def tell(semaphore, partners):
        for device in partners:
            pl.semaphore_signal(semaphore, inc=1, device_id=device, device_id_type=MESH)

    def tell_near(semaphore):
        tell(semaphore, near)
        for there, other in ((has_left, left), (has_right, right)):
            pl.when(there)(lambda other=other: tell(semaphore, [{"patch": other}]))

    def tell_round(n):
        if n < 2:
            tell_near(known.at[n])
        tell(known.at[n], far[n])

    def hear_round(n):
        pl.semaphore_wait(known.at[n], len(far[n]) + (near_count if n < 2 else 0))

    tell_near(barrier)

    def if_left(op):
        pl.when(has_left)(op)

    def if_right(op):
        pl.when(has_right)(op)

    @pl.when(p == 0)
    def _():
        kvw[0] = jnp.zeros((ROWS, 128), BF)
        halo_in[0] = jnp.zeros((ROWS, 128), BF)

    @pl.when(p == 31)
    def _():
        kvw[2] = jnp.zeros((ROWS, 128), BF)
        halo_in[1] = jnp.zeros((ROWS, 128), BF)


    def norm(i):
        rows = tile(i)
        x_load(i).wait()
        xs = x_ref[rows, :].astype(F32)
        inv = lax.rsqrt(jnp.sum(xs * xs, axis=1, keepdims=True) * (1.0 / D) + 1e-06)
        hid[rows, :] = (xs * inv * gain_ref[...]).astype(BF)
        irms[rows, :] = jnp.broadcast_to(inv, (TILE, 128))

    loads[0].wait()
    norm(0)

    for load in loads[1:]:
        load.wait()
    for to, at, size in ((0, 64, 128), (128, 0, 64), (192, 192, 64)):
        wt[to : to + size, :] = (
            pw_ref[at : at + size, :].astype(F32) + wn_ref[at : at + size, :].astype(F32)
        ).astype(BF)

    def halo_copy(side, i):
        return remote(
            kvw.at[1, tile(i), :], kvw.at[2 * side, tile(i), :],
            halo_s.at[side, i], halo_r.at[side, i], patch=left if side else right,
        )

    for i in range(3):
        rows = tile(i)
        pr = nt(hid[rows, :], wt[...])
        kvw[1, rows, :] = pr[:, :128].astype(BF)
        q_raw[rows, :] = pr[:, 128:].astype(BF)
        if i == 0:
            pl.semaphore_wait(barrier, near_count)
        if_right(halo_copy(0, i).start)
        if_left(halo_copy(1, i).start)
        if i < 2:
            norm(i + 1)
    tell_round(0)

    def queries(i, carry):
        rows = tile(i)
        lane = lax.broadcasted_iota(jnp.int32, (TILE, 128), 1)
        q = jnp.where(lane < 64, q_raw[rows, :].astype(F32), 0.0)
        qz[rows, :] = (q * 0.125).astype(BF)
        q_t[:, rows] = jnp.transpose(q)[:64, :].astype(BF)
        return carry

    lax.fori_loop(0, 3, queries, 0)

    lane12 = lax.broadcasted_iota(jnp.int32, (CAP, 128), 1)
    for load in small_loads:
        load.wait()
    nb = nb_ref[...]
    member = lane12 == 64 + nb[:, 0:1]
    for j in range(1, NB):
        member = member | (lane12 == 64 + nb[:, j : j + 1])
    member = jnp.where(member, 0.0, OFF)
    member = jnp.where(lane12 == 100, 1.0, jnp.where(lane12 > 100, 0.0, member))
    lane64 = lax.broadcasted_iota(jnp.int32, (PIX, 128), 1)
    for b, owner in enumerate((left, p, right)):
        valid = pltpu.roll(pv_ref[...], SLOTS - owner * CAP, 1)[:, :128]
        valid = jnp.where(valid > 0, 0.0, OFF)
        for s in range(CAP):
            aux = jnp.where(lane64 == 64 + b * CAP + s, 1.0, 0.0)
            aux = jnp.where(lane64 == 100, valid[:, s : s + 1], aux)
            kaug[b, s * PIX : (s + 1) * PIX, :] = aux.astype(BF)

    for load in late_loads:
        load.wait()
    live = counts_ref[p] * PIX
    for i in range(3):
        rows = tile(i)
        row = lax.broadcasted_iota(jnp.int32, (TILE, 1), 0) + i * TILE
        up[rows, :] = jnp.where(row < live, g_ref[rows, :].astype(F32), 0.0).astype(BF)
    og = nt(up[...], wt[128:256, :])
    lane = lax.broadcasted_iota(jnp.int32, (ROWS, 128), 1)
    dz[...] = jnp.where(lane >= 64, og, 0.0).astype(BF)
    for s in range(CAP):
        rows = slice(s * PIX, (s + 1) * PIX)
        qaug[rows, :] = jnp.where(lane64 < 64, qz[rows, :].astype(F32), member[s : s + 1, :]).astype(BF)

    def fold(value, op):
        return op(value.reshape(value.shape[0] // 8, 8, value.shape[1]), axis=0)

    def row(value):
        return jnp.max(value, axis=0, keepdims=True)

    def soften(b, start, size, group):
        rows = pl.ds(start, size)
        kv = kvw[b, rows, :].astype(F32)
        lane = lax.broadcasted_iota(jnp.int32, (size, 128), 1)
        kaug[b, rows, :] = jnp.where(lane < 64, kv, kaug[b, rows, :].astype(F32)).astype(BF)
        kvt[b, :, rows] = jnp.transpose(kv).astype(BF)
        for q in range(3):
            cols = tile(q)
            score = nt(kaug[b, rows, :], qaug[cols, :])
            top = row(fold(score, jnp.max))
            tops[group, :, cols] = jnp.broadcast_to(top, (8, TILE))
            total = jnp.zeros((8, TILE), F32)
            weighted = jnp.zeros((8, TILE), F32)
            prob_grad = nt(kvw[b, rows, :], dz[cols, :])
            for i in range(size // TILE):
                some = slice(i * TILE, (i + 1) * TILE)
                at = pl.ds(b * ROWS + start + i * TILE, TILE)
                e = jnp.exp(score[some, :] - top)
                sc[at, cols] = e
                dp[at, cols] = prob_grad[some, :]
                total = total + fold(e, jnp.sum)
                weighted = weighted + fold(e * prob_grad[some, :], jnp.sum)
            sums[group, 0, :, cols] = total
            sums[group, 1, :, cols] = weighted

    def divide_block(b, i, q, inv, delta):
        cols = tile(q)
        rows = tile(b * 3 + i)
        att = sc[rows, cols] * inv
        pt[rows, cols] = att.astype(BF)
        ds_t[rows, cols] = (att * (dp[rows, cols] - delta)).astype(BF)

    hear_round(0)
    tell_round(1)

    soften(1, 0, ROWS, 0)
    for i in range(3):
        for side in range(2):
            (if_right if side else if_left)(halo_copy(side, i).wait_recv)
            soften(2 * side, i * TILE, TILE, 1 + 2 * i + side)

    hear_round(1)
    tell_round(2)
    scales = []
    for q in range(3):
        cols = tile(q)
        group_tops = [tops[g, 0:1, cols] for g in range(7)]
        top = group_tops[0]
        for other in group_tops[1:]:
            top = jnp.maximum(top, other)
        shrink = [jnp.exp(other - top) for other in group_tops]
        total = jnp.zeros((8, TILE), F32)
        weighted = jnp.zeros((8, TILE), F32)
        for g in range(7):
            total = total + sums[g, 0, :, cols] * shrink[g]
            weighted = weighted + sums[g, 1, :, cols] * shrink[g]
        inv = 1.0 / jnp.sum(total, axis=0, keepdims=True)
        delta = jnp.sum(weighted, axis=0, keepdims=True) * inv
        scales.append(([inv * factor for factor in shrink], delta))

    def near_grad(start, size):
        at = pl.ds(start, size)
        return nn(ds_t[at, :], qz[...]) + nn(pt[at, :], dz[...])

    def grad_copy(side, i):
        return remote(
            halo_out.at[side, tile(i), :], halo_in.at[1 - side, tile(i), :],
            hg_s.at[side, i], hg_r.at[1 - side, i], patch=right if side else left,
        )

    chunks = [(side, i) for i in range(3) for side in range(2)]

    def divide_chunk(b, i):
        group = 0 if b == 1 else 1 + 2 * i + b // 2
        for q in range(3):
            divide_block(b, i, q, scales[q][0][group], scales[q][1])

    divide_chunk(0, 0)
    for n, (side, i) in enumerate(chunks):
        grads = near_grad((2 * side * 3 + i) * TILE, TILE)
        if n + 1 < len(chunks):
            divide_chunk(2 * chunks[n + 1][0], chunks[n + 1][1])
        halo_out[side, tile(i), :] = grads.astype(BF)
        (if_right if side else if_left)(grad_copy(side, i).start)

    for i in range(3):
        divide_chunk(1, i)
    own_grad[...] = near_grad(ROWS, ROWS)

    def query_side(q, carry):
        cols = tile(q)
        qg = jnp.zeros((64, TILE), F32)
        at = jnp.zeros((64, TILE), F32)
        for b in range(3):
            rows = slice(b * ROWS, (b + 1) * ROWS)
            qg = qg + nn(kvt[b, 0:64, :], ds_t[rows, cols])
            at = at + nn(kvt[b, 64:128, :], pt[rows, cols])
        grads_t[128:192, cols] = (qg * 0.125).astype(BF)
        att_t[:, cols] = at.astype(BF)
        return carry

    for q in range(3):
        query_side(q, 0)

    def put(h, n, value):
        for j in range(8):
            y, d = divmod(n * 8 + j, Z)
            pj[h, y, d % 4, (d // 4) * 32 : (d // 4) * 32 + 32, :] = value[j * 32 : j * 32 + 32, :]

    whole, first, last = slice(0, 128), slice(0, 64), slice(64, 128)
    window = [
        (1, 2, first), (1, 14, last), (0, 2, first), (0, 14, last),
        (1, 1, whole), (1, 15, whole), (1, 0, whole), (0, 1, whole), (0, 15, whole),
    ]

    def a_copy(h, n):
        other, step, rows = window[n]
        return remote(
            pj.at[h, 1 - y_lo if other else y_lo, (z + step) % 4, rows, :], a_in.at[h, n, rows, :],
            a_s.at[h, n], a_r.at[h, n], patch=z_peer(step, other),
        )

    def b_copy(h, r):
        return remote(
            b_out.at[h, tile((z // 4 + r) % 4, 32), :], b_in.at[h, r - 1],
            b_s.at[h, r - 1], b_r.at[h, r - 1], patch=z_peer(4 * r),
        )

    def a_stage(h):
        for n in range(9):
            a_copy(h, n).start()

    def b_stage(h):
        for n in range(9):
            a_copy(h, n).wait_recv()
        for i, rows in enumerate((first, last)):
            total = pj[h, y_lo, z % 4, rows, :].astype(F32)
            for n in (i, 2 + i, 4, 5, 6, 7, 8):
                total = total + a_in[h, n, rows, :].astype(F32)
            b_out[h, rows, :] = total.astype(BF)
        for r in (2, 1, 3):
            b_copy(h, r).start()

    def z_total(h):
        total = b_out[h, tile(z // 4, 32), :].astype(F32)
        for r in range(1, 4):
            b_copy(h, r).wait_recv()
            total = total + b_in[h, r - 1].astype(F32)
        for half in range(2):
            pg_ref[:, (1, 2)[half] if h else (0, 3)[half], :] = total[:, half * 64 : half * 64 + 64]

    for n in range(4):
        cols = tile(n)
        both = jnp.concatenate(
            [nn(grads_t[128:192, :], hid[:, cols]), nn(att_t[...], up[:, cols])], axis=0
        )
        put(0, n, jnp.transpose(both).astype(BF))
    hear_round(2)
    tell_round(3)
    a_stage(0)

    odd = core == 1
    share = pl.ds(pl.multiple_of((t // 2) * 128, 128), 128)

    def mine(value):
        turned = jnp.transpose(value)
        return jnp.where(odd, turned[64:, :], turned[:64, :])

    gain_share = mine(jnp.broadcast_to(gain_ref[:, share], (128, 128)))[:, :1]

    def shares(i, carry):
        rows = tile(i)
        inv = jnp.transpose(irms[rows, :])[:1, :]
        fscale[:, rows] = gain_share * inv
        nshare[:, rows] = mine(x_ref[rows, share].astype(F32)) * (inv * inv)
        ushare[:, rows] = mine(up[rows, share].astype(F32))
        return carry

    lax.fori_loop(0, 3, shares, 0)

    order = [(2, 0), (1, 0), (3, 0), (2, 1), (1, 1), (3, 1), (0, 0), (0, 1)]

    def block_of(o):
        dx, k = order[o]
        y = (1 - y_hi) if k == 0 else y_hi
        return y * NX + (x + dx) % NX

    for o in range(8):
        wk[o * 128 : (o + 1) * 128, :] = jnp.transpose(wt[:, tile(block_of(o), 128)].astype(F32)).astype(BF)


    def collect(i):
        rows = tile(i)
        for side in range(2):
            (if_left if side else if_right)(grad_copy(side, i).wait_recv)
        total = (
            own_grad[rows, :] + halo_in[0, rows, :].astype(F32) + halo_in[1, rows, :].astype(F32)
        )
        kvg = jnp.transpose(total).astype(BF)
        grads_t[0:128, rows] = kvg
        prod = jnp.sum(kvg.astype(F32) * kvt[1, :, rows].astype(F32), axis=0, keepdims=True)
        qg = grads_t[128:192, rows].astype(F32) * q_t[:, rows].astype(F32)
        prod = prod + jnp.sum(qg, axis=0, keepdims=True)
        for j in range(2):
            m_out[pl.ds(2 * i + j, 1), :] = prod[:, j * 128 : (j + 1) * 128]

    def core_copy(o):
        return remote(
            part.at[o, tile(1 - core, 64), :], r1.at[o], c_s.at[o], c_r.at[o], tensor=core_partner
        )

    def part_group(group):
        some = nn(wk[group * 512 : (group + 1) * 512, 0:192], grads_t[...])
        for n in range(4):
            o = group * 4 + n
            part[o] = some[n * 128 : (n + 1) * 128, :].astype(BF)
            core_copy(o).start()

    def pair_sum(o):
        core_copy(o).wait_recv()
        return part[o, tile(core, 64), :].astype(F32) + r1[o].astype(F32)

    def chip_copy(o):
        to = (t + 8) % 16 if o == 6 else row0 + (x + order[o][0]) % NX * 2
        return remote(s2.at[o], r2.at[o], r2_s.at[o], r2_r.at[o], tensor=to)

    def x_send(o):
        s2[o] = pair_sum(o).astype(BF)
        chip_copy(o).start()

    def x_sum(k):
        total = pair_sum(6 + k)
        for o in range(3 * k, 3 * k + 3):
            chip_copy(o).wait_recv()
            total = total + r2[o].astype(F32)
        return total

    m_out[...] = jnp.zeros_like(m_out)
    for i in range(2):
        collect(i)
    for n in range(4):
        cols = tile(n)
        w_acc[:, cols] = nn(grads_t[0:128, 0:512], hid[0:512, cols])
    collect(2)
    part_group(0)
    for n in range(4):
        cols = tile(n)
        total = w_acc[:, cols] + nn(grads_t[0:128, 512:768], hid[512:768, cols])
        put(1, n, jnp.transpose(total).astype(BF))
    a_stage(1)
    for o in range(3):
        x_send(o)
    part_group(1)

    def m_send(r, carry):
        remote(m_out, m_in.at[r - 1], m_s, m_r, tensor=(t + r) % 16).start()
        return carry

    lax.fori_loop(1, 16, m_send, 0)

    hear_round(3)
    b_stage(0)
    for o in (1, 2, 0):
        chip_copy(o).wait_send()
        x_send(o + 3)
    b_stage(1)
    s2[6] = x_sum(0).astype(BF)
    chip_copy(6).start()
    feature = x_sum(1)

    pltpu.make_async_copy(m_in, m_in, m_r).wait()
    m = m_out[...]
    for r in range(15):
        m = m + m_in[r]
    m = m * (1.0 / D)
    mean = jnp.concatenate([m[i : i + 1, :] for i in range(6)], axis=1)

    chip_copy(6).wait_recv()
    feature = feature + r2[6].astype(F32)
    og_ref[...] = (ushare[...] + feature * fscale[...] - nshare[...] * mean).astype(BF)
    z_total(0)
    z_total(1)

    for side in range(2):
        for i in range(3):
            (if_left if side else if_right)(halo_copy(side, i).wait_send)
            (if_right if side else if_left)(grad_copy(side, i).wait_send)
    for o in range(8):
        core_copy(o).wait_send()
    for o in range(3, 7):
        chip_copy(o).wait_send()
    for h in range(2):
        for n in range(9):
            a_copy(h, n).wait_send()
        for r in range(1, 4):
            b_copy(h, r).wait_send()
    pltpu.make_async_copy(m_in, m_in, m_s).wait()


def per_device(
    inputs, cotangent, norm_gain, proj_weight, weight_noise, patch_counts, neighbours, pixel_valid
):
    def turned(weight):
        return jnp.transpose(weight, (1, 2, 0)).reshape(4 * weight.shape[2], D)

    vmem = pl.BlockSpec(memory_space=pltpu.VMEM)
    hbm = pl.BlockSpec(memory_space=pl.ANY)
    V = pltpu.VMEM
    dma = pltpu.SemaphoreType.DMA
    grad, proj = pl.pallas_call(
        kernel,
        out_shape=(V((64, ROWS), BF), V((32, 4, 64), F32)),
        in_specs=[hbm] * 8,
        out_specs=(vmem, vmem),
        scratch_shapes=[
            V((ROWS, D), BF),
            V((ROWS, D), BF),
            V((1, D), F32),
            V((256, D), BF),
            V((256, D), BF),
            pltpu.SMEM((32,), jnp.int32),
            V((CAP, NB), jnp.int32),
            V((PIX, SLOTS), jnp.int32),
            V((256, D), BF),
            V((D, 256), BF),
            V((ROWS, D), BF),
            V((ROWS, D), BF),
            V((ROWS, 128), F32),
            V((64, ROWS), F32),
            V((64, ROWS), F32),
            V((64, ROWS), F32),
            V((3, ROWS, 128), BF),
            V((3, 128, ROWS), BF),
            V((3, ROWS, 128), BF),
            V((ROWS, 128), BF),
            V((ROWS, 128), BF),
            V((ROWS, 128), BF),
            V((ROWS, 128), BF),
            V((64, ROWS), BF),
            V((3 * ROWS, ROWS), F32),
            V((3 * ROWS, ROWS), F32),
            V((7, 8, ROWS), F32),
            V((7, 2, 8, ROWS), F32),
            V((3 * ROWS, ROWS), BF),
            V((3 * ROWS, ROWS), BF),
            V((2, ROWS, 128), BF),
            V((ROWS, 128), F32),
            V((2, ROWS, 128), BF),
            V((64, ROWS), BF),
            V((192, ROWS), BF),
            V((8, 128), F32),
            V((15, 8, 128), F32),
            V((2, 2, 4, 128, 128), BF),
            V((2, 9, 128, 128), BF),
            V((2, 128, 128), BF),
            V((2, 3, 32, 128), BF),
            V((8, 128, ROWS), BF),
            V((8, 64, ROWS), BF),
            V((7, 64, ROWS), BF),
            V((7, 64, ROWS), BF),
            V((128, D), F32),
            dma((3,)), dma, dma((6,)),
            dma((2, 3)), dma((2, 3)),
            dma((2, 3)), dma((2, 3)),
            dma, dma,
            dma((2, 9)), dma((2, 9)),
            dma((2, 3)), dma((2, 3)),
            dma((8,)), dma((8,)),
            dma((7,)), dma((7,)),
            pltpu.SemaphoreType.REGULAR((4,)),
        ],
        compiler_params=pltpu.CompilerParams(
            collective_id=0, has_side_effects=True, vmem_limit_bytes=56 * 1024 * 1024
        ),
        cost_estimate=pl.CostEstimate(
            flops=4 * 10**9, bytes_accessed=5 * 10**6, transcendentals=2 * 10**6
        ),
    )(
        inputs,
        cotangent,
        norm_gain.reshape(1, D),
        turned(proj_weight),
        turned(weight_noise),
        patch_counts,
        neighbours,
        jnp.transpose(pixel_valid),
    )
    return (jnp.transpose(grad), proj)


def solution(mesh):
    placed = (
        P("patch", None),
        P("patch", None),
        P(),
        P(None, None, "tensor"),
        P(None, None, "tensor"),
        P(),
        P("patch", None),
        P(),
    )
    return jax.shard_map(
        per_device,
        mesh=mesh,
        in_specs=placed,
        out_specs=(P("patch", "tensor"), P("patch", None, "tensor")),
        check_vma=False,
    )
```
